256 devices in a mesh: circ: 32 (over y_hi, z, core), axial: 8 (over y_lo, x).
Axes of the slice: x: 4, y: 4 (y_hi: 2, y_lo: 2; y = y_hi * 2 + y_lo), z: 8, core: 2. Of those that a mesh axis runs over, the one named last changes fastest.
Arguments:
- scanned: float32 [3, 512, 32, 2048], P(None, None, 'circ', 'axial'), may hold values from -12 to 12
- block_mask: int32 [128, 16], P('circ', 'axial'), may hold values 0 or 1
Outputs:
- solution: float32 [3, 8192, 1024], P(None, 'circ', 'axial')
- residual: float32 [3, 8192, 1024], P(None, 'circ', 'axial')
The draws below stay inside these ranges and needn't reach their ends.
All inputs are finite; a program needn't handle non-finite values. No bound on the sum of `block_mask` on one device may be relied on, other than what follows from the above.
Results may differ from the reference program's by a relative error of at most 0.00017.
Values sent between devices are 32-bit elements; how exact they have to be, the bound alone decides.
No kernel may reach another device: no remote copies, remote signals or barrier semaphores. Data moves between devices by JAX's collectives and lax.ppermute only.
A program may use at most 64 MiB of HBM per device.

```python
import jax
import jax.numpy as jnp
from jax import lax

BLK = 128
ITERS = 2
SRD = 512
SC = 16384
SA = 2048
N_CIRC = 32


def draw_scanned(key, part):
    key = jax.random.fold_in(key, 11)
    row_index = (jnp.arange(SRD)[:, None] * N_CIRC + jnp.arange(N_CIRC)[None, :]).astype(jnp.float32)
    rising = 1.0 + 2.0 * row_index / (SRD * N_CIRC)
    base = jax.random.normal(key, (3, SRD, N_CIRC, SA), jnp.float32)
    values = jnp.clip(base, -4.0, 4.0) * rising[None, :, :, None]
    return values


def set_ends(array, stream_key, smallest, largest):
    dims = array.shape
    place = [jax.random.randint(jax.random.fold_in(stream_key, axis), (), 0, dims[axis]) for axis in range(len(dims))]
    array = array.at[tuple(place)].set(smallest)
    longest = dims.index(max(dims))
    place[longest] = (place[longest] + 1) % dims[longest]
    return array.at[tuple(place)].set(largest)


def setup_inputs(seed: int = 0) -> dict:
    seeds = jax.random.split(jax.random.key(seed), 3)
    scanned = draw_scanned(jax.random.fold_in(seeds[2], 71), 0)
    block_mask = set_ends((jax.random.randint(seeds[1], (SC // BLK, SA // BLK), 0, 4) < 3).astype(jnp.int32), jax.random.fold_in(seeds[1], 1), 0, 1)
    return dict(scanned=scanned, block_mask=block_mask)


ridge_weight = 0.05


def spread(padded, axis):
    length = padded.shape[axis] - 3
    tap_zero = lax.slice_in_dim(padded, 0, length, axis=axis)
    tap_one = lax.slice_in_dim(padded, 1, length + 1, axis=axis)
    tap_two = lax.slice_in_dim(padded, 2, length + 2, axis=axis)
    tap_three = lax.slice_in_dim(padded, 3, length + 3, axis=axis)
    at_knots = (tap_zero + 4.0 * tap_one + tap_two) / 6.0
    at_halves = (tap_zero + 23.0 * tap_one + 23.0 * tap_two + tap_three) / 48.0
    joined = jnp.stack([at_knots, at_halves], axis=axis + 1)
    dims_list = list(padded.shape)
    dims_list[axis] = 2 * length
    return joined.reshape(dims_list)


def collect(padded, axis):
    length = padded.shape[axis] // 2 - 3
    dims_list = list(padded.shape)
    dims_list[axis:axis + 1] = [length + 3, 2]
    paired = padded.reshape(dims_list)
    halves_at = lax.index_in_dim(paired, 0, axis + 1, keepdims=False)
    knots_at = lax.index_in_dim(paired, 1, axis + 1, keepdims=False)

    def window(values, offset):
        return lax.slice_in_dim(values, offset, offset + length, axis=axis)

    return ((window(halves_at, 0) + window(halves_at, 3)) / 48.0
            + (window(knots_at, 0) + window(knots_at, 2)) / 6.0
            + 23.0 * (window(halves_at, 1) + window(halves_at, 2)) / 48.0
            + 4.0 * window(knots_at, 1) / 6.0)


def adjoint(masked):
    padded = jnp.pad(masked, ((3, 3), (0, 0)), mode="wrap")
    padded = jnp.pad(padded, ((0, 0), (3, 3)))
    return collect(collect(padded, 0), 1)


def apply_normal(control, weights):
    padded = jnp.pad(control, ((2, 2), (0, 0)), mode="wrap")
    padded = jnp.pad(padded, ((0, 0), (2, 2)))
    surface = spread(padded, 0)[2:2 + SC]
    surface = spread(surface, 1)[:, 2:2 + SA]
    return adjoint(surface * weights) + ridge_weight * control


def reference(scanned, block_mask):
    samples = scanned.reshape(3, SC, SA)
    weights = jnp.repeat(jnp.repeat(block_mask.astype(jnp.float32), BLK, axis=0), BLK, axis=1)

    def operate(control):
        return lax.map(lambda single: apply_normal(single, weights), control)

    right_side = lax.map(lambda single: adjoint(single * weights), samples)
    solution = jnp.zeros_like(right_side)
    residual = right_side
    direction = right_side
    norm_now = jnp.sum(residual * residual)
    for iteration in range(ITERS):
        applied = operate(direction)
        step_size = norm_now / jnp.sum(direction * applied)
        solution = solution + step_size * direction
        residual = residual - step_size * applied
        norm_next = jnp.sum(residual * residual)
        direction = residual + (norm_next / norm_now) * direction
        norm_now = norm_next
    return solution, residual
```

```python
import functools

import jax
import jax.numpy as jnp
import numpy as np
from jax import lax
from jax.experimental import pallas as pl
from jax.experimental.pallas import tpu as pltpu
from jax.sharding import PartitionSpec as P

ridge_weight = 0.05
KS = 3
QN = 32
AN = 8
SL = 16
PR = 56
ROWS = 288
PAD = 16
LO, HI = 8, 280
LS, LB = 144, 8
VMEM_LIMIT = 48 * 1024 * 1024
F32 = jnp.float32
BF16 = jnp.bfloat16

TAPS = {0: 32.0, 1: 23.0, 2: 8.0, 3: 1.0}


def column_matrix():
    full = np.zeros((256, 256), np.float32)
    for a in range(128):
        for j in range(256):
            tap = TAPS.get(abs(j - 2 * a), 0.0)
            if tap and not (a in (63, 64, 65) and j >= 128):
                full[j, a] = tap
    for e, (a, low, high) in enumerate(
        [(-1, 0, 128), (128, 128, 256), (129, 128, 256), (63, 128, 256), (64, 128, 256), (65, 128, 256)]
    ):
        for j in range(low, high):
            for h in range(2):
                full[j, 128 + 18 * h + e] = TAPS.get(abs(j - 2 * a), 0.0)
    return full


def lanes(rows):
    return lax.broadcasted_iota(jnp.int32, (rows, 128), 1)


def roll(x, shift, axis=1):
    shift = shift % x.shape[axis]
    return x if shift == 0 else pltpu.roll(x, shift, axis)


def split_dot(x, matrix):
    high = x.astype(BF16)
    rest = x - high.astype(F32)
    mid = rest.astype(BF16)
    low = (rest - mid.astype(F32)).astype(BF16)
    dot = functools.partial(jnp.dot, preferred_element_type=F32)
    return dot(low, matrix) + dot(mid, matrix) + dot(high, matrix)


def pack_kernel(mask_ref, x_ref, c_ref, out_ref, main_ref, ext_ref):
    q = lax.axis_index("circ")
    lane = lanes(QN)
    matrix = c_ref[...]
    tile = None
    ext17 = None
    next_rows = []
    for k in range(KS):
        left = x_ref[k, pl.ds(0, 512, stride=2), :]
        right = x_ref[k, pl.ds(1, 512, stride=2), :]
        both = split_dot(jnp.concatenate([left, right], axis=1), matrix)
        main_ref[...] = both[:, :128]
        ext_ref[...] = both[:, 128:]
        for d in range(QN):
            out_ref[pl.ds(d * PR + k * SL, SL), :] = both[d * SL : (d + 1) * SL, :128]
        ext = both[:, 128:].reshape(QN, 2, 8, 128)
        ext = jnp.where(lanes(QN * 8) < 18, ext[:, 0].reshape(QN * 8, 128), ext[:, 1].reshape(QN * 8, 128))
        ext = roll(ext, 6 * k)
        tile = ext if tile is None else tile + ext

        def neighbour(ref):
            first = ref[pl.ds(0, QN, stride=SL), :]
            last = ref[pl.ds(SL - 1, QN, stride=SL), :]
            return jnp.where(q >= QN // 2, roll(last, 1, 0), roll(first, -1, 0))

        next_rows.append(neighbour(main_ref))
        ext_row = roll(jnp.where(lane < 6, neighbour(ext_ref), 0.0), 6 * k)
        ext17 = ext_row if ext17 is None else ext17 + ext_row
    for d in range(QN):
        out_ref[pl.ds(d * PR + 48, 8), :] = tile[d * 8 : (d + 1) * 8]
    mask_row = jnp.zeros((QN, 128), F32)
    for row in range(4):
        for col in range(2):
            mask_row = jnp.where(lane == 64 + 2 * row + col, mask_ref[row, col].astype(F32), mask_row)
    fill = []
    for k in range(KS):
        fill += [roll(next_rows[k], 64), next_rows[k]]
    fill += [roll(ext17, 64), mask_row]
    for row in range(8):
        where = pl.ds(48 + row, QN, stride=PR)
        out_ref[where, :] = jnp.where(lane < 64, out_ref[where, :], fill[row])


def tap_rows(even, odd, start, size):
    def ev(offset):
        return even(start + offset, size)

    def od(offset):
        return odd(start + offset, size)

    return (
        32.0 * ev(0) + 8.0 * (ev(-1) + ev(1)) + 23.0 * (od(-1) + od(0)) + (od(-2) + od(1))
    )


def block_row_ranges():
    edges = [LO] + [PAD + 64 * b for b in range(5)] + [HI]
    return list(zip(edges[:-1], edges[1:]))


def collect_kernel(mask_ref, got_ref, b_ref, right_ref, left_ref, m_ref, even_ref, odd_ref):
    d = lax.axis_index("circ")
    row_lane = lanes(1)

    def spread_lane(x, at):
        return jnp.broadcast_to(x[:, at : at + 1], (1, 128))

    before = got_ref[pl.ds(lax.rem(d + QN - 1, QN) * PR + 55, 1), :]
    after = got_ref[pl.ds(lax.rem(d + 1, QN) * PR + 55, 1), :]
    weights = [(spread_lane(before, 70), spread_lane(before, 71))]
    for row in range(4):
        weights.append(tuple(jnp.full((1, 128), mask_ref[row, col].astype(F32)) for col in range(2)))
    weights.append((spread_lane(after, 64), spread_lane(after, 65)))
    main_w = [jnp.where(row_lane <= 65, low, high) for low, high in weights]
    ext_first = (row_lane == 0) | (row_lane == 6) | (row_lane == 12)
    ext_w = [jnp.where(ext_first, low, high) for low, high in weights]
    zeros = jnp.zeros((8, 128), F32)
    for ref in (even_ref, odd_ref):
        for t in range(4):
            ref[t, 0:8, :] = zeros
            ref[t, HI : HI + 8, :] = zeros
    for parity, ref in ((0, even_ref), (1, odd_ref)):
        for k in range(KS):
            for s in range(SL):
                rows = got_ref[pl.ds(parity * PR + k * SL + s, 16, stride=2 * PR), :]
                ref[k, PAD + 16 * s : PAD + 16 * s + 16, :] = rows * main_w[1 + s // 4]
            low = got_ref[pl.ds(parity * PR + 48 + 2 * k, 16, stride=2 * PR), :]
            high = got_ref[pl.ds(parity * PR + 49 + 2 * k, 16, stride=2 * PR), :]
            rows = jnp.where(lanes(16) < 64, roll(low, 64), high)
            ref[k, HI - 8 : HI, :] = rows[:8] * main_w[5]
            ref[k, LO : LO + 8, :] = rows[8:] * main_w[0]
        for r in range(8):
            rows = got_ref[pl.ds(parity * PR + 48 + r, 16, stride=2 * PR), :]
            ref[3, PAD + 16 * r : PAD + 16 * r + 16, :] = rows * ext_w[1 + r // 4]
            at = PAD + 128 + 16 * r
            ref[3, at : at + 16, :] = roll(rows, -18) * ext_w[3 + r // 4]
        rows = roll(got_ref[pl.ds(parity * PR + 54, 16, stride=2 * PR), :], 64)
        ref[3, HI - 8 : HI, :] = rows[:8] * ext_w[5]
        ref[3, LO : LO + 8, :] = rows[8:] * ext_w[0]
    scale = 1.0 / (48.0 * 48.0)
    for t in range(4):
        b_ref[t, 0:8, :] = zeros
        b_ref[t, HI : HI + 8, :] = zeros
        for start in range(LO, HI, 16):
            b_ref[t, start : start + 16, :] = scale * tap_rows(
                lambda at, size: even_ref[t, at : at + size, :],
                lambda at, size: odd_ref[t, at : at + size, :],
                start,
                16,
            )
    lane8 = lanes(8)
    mask_cols = jnp.zeros((8, 128), F32)
    sub8 = lax.broadcasted_iota(jnp.int32, (8, 128), 0)
    for row in range(6):
        for col in range(2):
            mask_cols = jnp.where((sub8 == row) & (lane8 == 24 + col), weights[row][col], mask_cols)
    m_ref[...] = mask_cols
    for ref, to_right in ((right_ref, True), (left_ref, False)):
        lane = lanes(72)
        packed = None
        for g in range(4):
            rows = slice(72 * g, 72 * g + 72)
            ext = b_ref[3, rows, :]
            piece = jnp.zeros((72, 128), F32)
            for k in range(KS):
                main = b_ref[k, rows, :]
                if to_right:
                    first, second = roll(main, 8 * k - 122), roll(ext, 2 * k + 5)
                    cut = 8 * k + 6
                else:
                    first, second = roll(ext, 2 * k), roll(main, 8 * k + 1)
                    cut = 8 * k + 1
                piece = jnp.where((lane >= 8 * k) & (lane < 8 * k + 8), jnp.where(lane < cut, first, second), piece)
            if g == 0:
                piece = piece + jnp.concatenate([mask_cols, jnp.zeros((64, 128), F32)], axis=0)
            piece = roll(piece, 32 * g)
            packed = piece if packed is None else packed + piece
        ref[...] = packed


def place_kernel(b_ref, out_ref):
    for start in range(0, ROWS, 16):
        rows = slice(start, start + 16)
        lane = lanes(16)
        ext = b_ref[3, rows, :]
        rolled = []
        for k in range(KS):
            main = b_ref[k, rows, :]
            middle = roll(ext, 63 - (6 * k + 3))
            main = main + jnp.where((lane >= 63) & (lane < 66), middle, 0.0)
            rolled.append(roll(main, LB + 16 * k))
        for t in range(4):
            out = jnp.zeros((16, 128), F32)
            if t < KS:
                off = LB + 16 * t
                out = jnp.where(lane >= off, rolled[t], out)
                out = jnp.where(lane == off - 1, roll(ext, off - 1 - 6 * t), out)
            if t > 0:
                k = t - 1
                off = LB + 16 * k
                out = jnp.where(lane < off, rolled[k], out)
                out = jnp.where((lane >= off) & (lane < off + 2), roll(ext, off - (6 * k + 1)), out)
            out_ref[t, rows, :] = out


def lane_shift(parts, shift):
    rolled = [roll(part, -shift) for part in parts]
    lane = lanes(parts[0].shape[0])
    count = len(parts)
    if shift < 0:
        return [jnp.where(lane < -shift, rolled[(t - 1) % count], rolled[t]) for t in range(count)]
    return [jnp.where(lane >= 128 - shift, rolled[(t + 1) % count], rolled[t]) for t in range(count)]


def packed_columns(t):
    out = []
    for lane in range(128):
        at = 128 * t + lane
        k = min(at // LS, KS - 1)
        out.append(at - k * LS - LB)
    return out


def lane_range(lane, t, low, high):
    columns = packed_columns(t)
    where = None
    at = 0
    while at < 128:
        if low <= columns[at] < high:
            end = at
            while end < 128 and low <= columns[end] < high:
                end += 1
            piece = (lane >= at) & (lane < end)
            where = piece if where is None else where | piece
            at = end
        else:
            at += 1
    return where


def choose(where, x, y):
    return y if where is None else jnp.where(where, x, y)


def operate_kernel(
    own_ref, m_ref, from_left_ref, from_right_ref, red_ref, b_ref, p_ref, s_ref, ve_ref, vo_ref, x_ref, w_ref
):
    place = lax.axis_index("axial")
    inner_left = (place > 0).astype(F32)
    inner_right = (place < AN - 1).astype(F32)
    lane8 = lanes(8)
    lane16 = lanes(16)
    ones = jnp.ones((8, 128), F32)
    inside = []
    main = []
    for t in range(4):
        keep = choose(lane_range(lane8, t, -8, 0), ones * inner_left, ones)
        inside.append(choose(lane_range(lane8, t, 128, 200), ones * inner_right, keep))
        main.append(choose(lane_range(lane8, t, 0, 128), ones, jnp.zeros((8, 128), F32)))
    scale = 1.0 / (48.0**4)
    for block in range(6):

        def cell(ref, at):
            return jnp.broadcast_to(ref[block : block + 1, at : at + 1], (8, 128)) * scale

        low, high = cell(m_ref, 24), cell(m_ref, 25)
        left, right = cell(from_left_ref, 25), cell(from_right_ref, 24)
        for t in range(4):
            value = choose(lane_range(lane8, t, -8, 0), left, right)
            value = choose(lane_range(lane8, t, 0, 64), low, value)
            w_ref[t, 8 * block : 8 * block + 8, :] = choose(lane_range(lane8, t, 64, 128), high, value)

    for g in range(4):
        for start in range(72 * g, 72 * g + 72, 24):
            rows = slice(start, start + 24)
            there = slice(start - 72 * g, start - 72 * g + 24)
            lane = lanes(24)
            from_left, from_right = from_left_ref[there, :], from_right_ref[there, :]
            for t in range(4):
                out = own_ref[t, rows, :]
                if t < KS:
                    at = 2 + 16 * t
                    piece = roll(from_left, at - 8 * t - 32 * g)
                    out = out + jnp.where((lane >= at) & (lane < at + 8), piece, 0.0)
                if t > 0:
                    k = t - 1
                    at = 7 + 16 * k
                    piece = roll(from_right, at - 8 * k - 32 * g)
                    out = out + jnp.where((lane >= at) & (lane < at + 7), piece, 0.0)
                keep = jnp.concatenate([inside[t]] * 3, axis=0)
                b_ref[t, rows, :] = out * keep

    zeros = jnp.zeros((8, 128), F32)
    for t in range(4):
        for ref in (ve_ref, vo_ref, p_ref):
            ref[t, 0:8, :] = zeros
            ref[t, HI : HI + 8, :] = zeros
        for n in range(4):
            x_ref[n, t, 0:8, :] = zeros
            x_ref[n, t, HI : HI + 8, :] = zeros

    def weight_row(start):
        for block, (low, high) in enumerate(block_row_ranges()):
            if low <= start < high:
                return block
        return None

    def operate(src_ref, dst_ref, low, high, dst_shift):
        for start in range(LO, HI, 8):
            rows = slice(start, start + 8)
            v = [src_ref[t, rows, :] for t in range(4)]
            before, after, second = lane_shift(v, -1), lane_shift(v, 1), lane_shift(v, 2)
            for t in range(4):
                ve_ref[t, rows, :] = 32.0 * v[t] + 8.0 * (before[t] + after[t])
                vo_ref[t, rows, :] = (before[t] + second[t]) + 23.0 * (v[t] + after[t])
        for n, ref in enumerate((ve_ref, vo_ref)):
            for t in range(4):
                for start in range(LO, HI, 8):
                    rows = slice(start, start + 8)
                    block = weight_row(start)
                    weight = w_ref[t, 8 * block : 8 * block + 8, :]
                    before = ref[t, start - 1 : start + 7, :]
                    here = ref[t, rows, :]
                    after = ref[t, start + 1 : start + 9, :]
                    second = ref[t, start + 2 : start + 10, :]
                    x_ref[2 * n, t, rows, :] = (32.0 * here + 8.0 * (before + after)) * weight
                    x_ref[2 * n + 1, t, rows, :] = ((before + second) + 23.0 * (here + after)) * weight
        for start in range(low, high, 8):
            rows = slice(start, start + 8)
            y = []
            for n in range(2):
                y.append(
                    [
                        tap_rows(
                            lambda at, size: x_ref[2 * n, t, at : at + size, :],
                            lambda at, size: x_ref[2 * n + 1, t, at : at + size, :],
                            start,
                            8,
                        )
                        for t in range(4)
                    ]
                )
            even, odd = y
            odd_before = lane_shift(odd, -1)
            first = [8.0 * even[t] + 23.0 * odd[t] + odd_before[t] for t in range(4)]
            first = lane_shift(first, -1)
            last = lane_shift([8.0 * even[t] + odd[t] for t in range(4)], 1)
            for t in range(4):
                total = 32.0 * even[t] + 23.0 * odd[t] + first[t] + last[t]
                value = (total + ridge_weight * src_ref[t, rows, :]) * inside[t]
                dst_ref[t, start - dst_shift : start - dst_shift + 8, :] = value

    operate(b_ref, p_ref, LO, HI, 0)
    operate(p_ref, s_ref, PAD, PAD + 256, PAD)

    def total(x):
        return jnp.sum(jnp.sum(x, axis=0, keepdims=True), axis=1, keepdims=True)

    sums = [zeros, zeros]
    for t in range(4):
        for start in range(PAD, PAD + 256, 8):
            b = b_ref[t, start : start + 8, :] * main[t]
            p = p_ref[t, start : start + 8, :]
            sums = [sums[0] + b * b, sums[1] + b * p]
    norm, moment = total(sums[0]), total(sums[1])
    shift = jnp.where(norm > 1e-30, moment / jnp.where(norm > 1e-30, norm, 1.0), 0.0)
    shift8 = jnp.broadcast_to(shift, (8, 128))
    sums = [zeros] * 4
    for t in range(4):
        for start in range(PAD, PAD + 256, 8):
            b = b_ref[t, start : start + 8, :] * main[t]
            p = p_ref[t, start : start + 8, :] * main[t]
            s = s_ref[t, start - PAD : start - PAD + 8, :]
            w = p - shift8 * b
            z = s - shift8 * p
            sums = [sums[0] + w * b, sums[1] + w * w, sums[2] + w * z, sums[3] + b * z]
    values = [norm, moment] + [total(x) for x in sums] + [shift]
    row_lane = lax.broadcasted_iota(jnp.int32, (1, 8), 1)
    row = jnp.zeros((1, 8), F32)
    for n, value in enumerate(values):
        row = jnp.where(row_lane == n, jnp.broadcast_to(value, (1, 8)), row)
    red_ref[...] = jnp.broadcast_to(row, red_ref.shape)


def unpack_kernel(b_ref, p_ref, s_ref, bm_ref, pm_ref, sm_ref):
    for src, dst, base in ((b_ref, bm_ref, PAD), (p_ref, pm_ref, PAD), (s_ref, sm_ref, 0)):
        for k in range(KS):
            off = LB + 16 * k
            for start in range(0, 256, 16):
                first = src[k, base + start : base + start + 16, :]
                second = src[k + 1, base + start : base + start + 16, :]
                both = jnp.where(lanes(16) >= off, first, second)
                dst[k, start : start + 16, :] = roll(both, -off)


def finish_kernel(red_ref, b_ref, p_ref, s_ref, sol_ref, res_ref):
    red = red_ref[...]
    norm, moment, c, v, wz, bz, mu = (red[:, n : n + 1] for n in range(7))

    def total(x):
        return jnp.sum(x, axis=0, keepdims=True)

    norm_now = total(norm)
    moment_all = total(moment)
    step = norm_now / moment_all
    shift = mu - moment_all / norm_now
    norm_next = step * step * total(v + 2.0 * shift * c + shift * shift * norm)
    beta = norm_next / norm_now
    r_ar = step * step * total(wz + shift * (v + mu * c + bz) + shift * shift * moment)
    cross = -step * total(bz + v + mu * c + 2.0 * shift * moment)
    curve = r_ar + beta * cross + beta * beta * moment_all
    step_two = norm_next / curve
    one_beta = 1.0 + beta

    def wide(x):
        return jnp.broadcast_to(x, (16, 128))

    step_b, step_two_b, one_beta_b = wide(step), wide(step_two), wide(one_beta)
    for k in range(KS):
        for start in range(0, 256, 16):
            rows = slice(start, start + 16)
            b, p, s = b_ref[k, rows, :], p_ref[k, rows, :], s_ref[k, rows, :]
            first = step_b * p
            sol_ref[k, rows, :] = step_b * b + step_two_b * (one_beta_b * b - first)
            res_ref[k, rows, :] = (b - first) - step_two_b * (one_beta_b * p - step_b * s)


def call(kernel, outs, scratch=(), smem=0, n_in=1, cost=None):
    vmem = pl.BlockSpec(memory_space=pltpu.VMEM)
    smem_spec = pl.BlockSpec(memory_space=pltpu.SMEM)
    return pl.pallas_call(
        kernel,
        out_shape=[jax.ShapeDtypeStruct(shape, F32) for shape in outs],
        in_specs=[smem_spec] * smem + [vmem] * (n_in - smem),
        out_specs=[vmem] * len(outs),
        scratch_shapes=[pltpu.VMEM(shape, F32) for shape in scratch],
        compiler_params=pltpu.CompilerParams(vmem_limit_bytes=VMEM_LIMIT),
        cost_estimate=cost,
    )


def shards(scanned, block_mask):
    matrix = jnp.asarray(column_matrix(), BF16)
    x = scanned.reshape(KS, 1024, 128)
    (packed,) = call(pack_kernel, [(QN * PR, 128)], [(512, 128), (512, 128)], smem=1, n_in=3)(
        block_mask, x, matrix
    )
    got = lax.all_to_all(packed.reshape(QN, PR, 128), "circ", 0, 0, tiled=True).reshape(QN * PR, 128)
    b_own, to_right, to_left, mask_cols = call(
        collect_kernel,
        [(4, ROWS, 128), (72, 128), (72, 128), (8, 128)],
        [(4, ROWS, 128), (4, ROWS, 128)],
        smem=1,
        n_in=2,
    )(block_mask, got)
    from_left = lax.ppermute(to_right, "axial", [(i, i + 1) for i in range(AN - 1)])
    from_right = lax.ppermute(to_left, "axial", [(i + 1, i) for i in range(AN - 1)])
    cost = pl.CostEstimate(flops=2_000_000, bytes_accessed=4_000_000, transcendentals=0)
    (own,) = call(place_kernel, [(4, ROWS, 128)], n_in=1, cost=cost)(b_own)
    red, b, p, s = call(
        operate_kernel,
        [(QN * AN, 8), (4, ROWS, 128), (4, ROWS, 128), (4, 256, 128)],
        [(4, ROWS, 128), (4, ROWS, 128), (4, 4, ROWS, 128), (4, 48, 128)],
        n_in=4,
    )(own, mask_cols, from_left, from_right)
    all_red = lax.all_to_all(red, ("circ", "axial"), 0, 0, tiled=True)
    bm, pm, sm = call(unpack_kernel, [(KS, 256, 128)] * 3, n_in=3, cost=cost)(b, p, s)
    return tuple(call(finish_kernel, [(KS, 256, 128)] * 2, n_in=4)(all_red, bm, pm, sm))


def solution(mesh):
    return jax.shard_map(
        shards,
        mesh=mesh,
        in_specs=(P(None, None, "circ", "axial"), P("circ", "axial")),
        out_specs=(P(None, "circ", "axial"), P(None, "circ", "axial")),
        check_vma=False,
    )
```

```python
import functools

import jax
import jax.numpy as jnp
from jax import lax
from jax.experimental import pallas as pl
from jax.experimental.pallas import tpu as pltpu
from jax.sharding import PartitionSpec as P

ridge_weight = 0.05
KS = 3
QN = 32
AN = 8
SL = 16
PR = 56
ROWS = 288
PAD = 16
LO, HI = 8, 280
LS, LB = 144, 8
VMEM_LIMIT = 48 * 1024 * 1024
F32 = jnp.float32
BF16 = jnp.bfloat16


def column_matrix():
    sample = lax.broadcasted_iota(jnp.int32, (256, 256), 0)
    out = lax.broadcasted_iota(jnp.int32, (256, 256), 1)
    extra = out - 128
    extra = jnp.where(extra >= 18, extra - 18, extra)
    center = jnp.where(extra == 0, -2, jnp.where(extra < 3, 254 + 2 * extra, 120 + 2 * extra))
    center = jnp.where(out < 128, 2 * out, jnp.where(extra < 6, center, 1000))
    inner = (out >= 63) & (out <= 65) & (sample >= 128)
    outer = (out >= 128) & (extra >= 3) & (sample < 128)
    apart = inner | outer
    away = jnp.abs(sample - center)
    taps = jnp.where(away == 0, 32.0, jnp.where(away == 1, 23.0, jnp.where(away == 2, 8.0, 1.0)))
    return jnp.where((away > 3) | apart, 0.0, taps).astype(BF16)


def lanes(rows):
    return lax.broadcasted_iota(jnp.int32, (rows, 128), 1)


def roll(x, shift, axis=1):
    shift = shift % x.shape[axis]
    return x if shift == 0 else pltpu.roll(x, shift, axis)


def split_dot(x, matrix):
    high = x.astype(BF16)
    rest = x - high.astype(F32)
    mid = rest.astype(BF16)
    low = (rest - mid.astype(F32)).astype(BF16)
    dot = functools.partial(jnp.dot, preferred_element_type=F32)
    return dot(low, matrix) + dot(mid, matrix) + dot(high, matrix)


def pack_kernel(mask_hbm, x_hbm, out_ref, mask_ref, x_ref, main_ref, ext_ref, sems):
    q = lax.axis_index("circ")
    copies = [pltpu.make_async_copy(x_hbm.at[k], x_ref.at[k], sems.at[k]) for k in range(KS)]
    copies.append(pltpu.make_async_copy(mask_hbm, mask_ref, sems.at[KS]))
    for copy in copies:
        copy.start()
    lane = lanes(QN)
    matrix = column_matrix()
    tile = None
    ext17 = None
    next_rows = []
    for k in range(KS):
        copies[k].wait()
        left = x_ref[k, pl.ds(0, 512, stride=2), :]
        right = x_ref[k, pl.ds(1, 512, stride=2), :]
        both = split_dot(jnp.concatenate([left, right], axis=1), matrix)
        main_ref[...] = both[:, :128]
        ext_ref[...] = both[:, 128:]
        for d in range(QN):
            out_ref[pl.ds(d * PR + k * SL, SL), :] = both[d * SL : (d + 1) * SL, :128]
        ext = both[:, 128:].reshape(QN, 2, 8, 128)
        ext = jnp.where(lanes(QN * 8) < 18, ext[:, 0].reshape(QN * 8, 128), ext[:, 1].reshape(QN * 8, 128))
        ext = roll(ext, 6 * k)
        tile = ext if tile is None else tile + ext

        def neighbour(ref):
            first = ref[pl.ds(0, QN, stride=SL), :]
            last = ref[pl.ds(SL - 1, QN, stride=SL), :]
            return jnp.where(q >= QN // 2, roll(last, 1, 0), roll(first, -1, 0))

        next_rows.append(neighbour(main_ref))
        ext_row = roll(jnp.where(lane < 6, neighbour(ext_ref), 0.0), 6 * k)
        ext17 = ext_row if ext17 is None else ext17 + ext_row
    for d in range(QN):
        out_ref[pl.ds(d * PR + 48, 8), :] = tile[d * 8 : (d + 1) * 8]
    copies[KS].wait()
    mask = mask_ref[...].astype(F32)
    mask_row = jnp.zeros((1, 128), F32)
    for row in range(4):
        for col in range(2):
            value = jnp.broadcast_to(mask[col : col + 1, row : row + 1], (1, 128))
            mask_row = jnp.where(lanes(1) == 64 + 2 * row + col, value, mask_row)
    mask_row = jnp.broadcast_to(mask_row, (QN, 128))
    fill = []
    for k in range(KS):
        fill += [roll(next_rows[k], 64), next_rows[k]]
    fill += [roll(ext17, 64), mask_row]
    for row in range(8):
        where = pl.ds(48 + row, QN, stride=PR)
        out_ref[where, :] = jnp.where(lane < 64, out_ref[where, :], fill[row])


def tap_rows(even, odd, start, size):
    def ev(offset):
        return even(start + offset, size)

    def od(offset):
        return odd(start + offset, size)

    return (
        32.0 * ev(0) + 8.0 * (ev(-1) + ev(1)) + 23.0 * (od(-1) + od(0)) + (od(-2) + od(1))
    )


def block_row_ranges():
    edges = [LO] + [PAD + 64 * b for b in range(5)] + [HI]
    return list(zip(edges[:-1], edges[1:]))


def collect_kernel(got_ref, b_ref, right_ref, left_ref, m_ref, even_ref, odd_ref):
    d = lax.axis_index("circ")
    row_lane = lanes(1)

    def spread_lane(x, at):
        return jnp.broadcast_to(x[:, at : at + 1], (1, 128))

    before = got_ref[pl.ds(lax.rem(d + QN - 1, QN) * PR + 55, 1), :]
    after = got_ref[pl.ds(lax.rem(d + 1, QN) * PR + 55, 1), :]
    weights = [(spread_lane(before, 70), spread_lane(before, 71))]
    mine = got_ref[pl.ds(d * PR + 55, 1), :]
    for row in range(4):
        weights.append(tuple(spread_lane(mine, 64 + 2 * row + col) for col in range(2)))
    weights.append((spread_lane(after, 64), spread_lane(after, 65)))
    main_w = [jnp.where(row_lane <= 65, low, high) for low, high in weights]
    ext_first = (row_lane == 0) | (row_lane == 6) | (row_lane == 12)
    ext_w = [jnp.where(ext_first, low, high) for low, high in weights]
    zeros = jnp.zeros((8, 128), F32)
    for ref in (even_ref, odd_ref):
        for t in range(4):
            ref[t, 0:8, :] = zeros
            ref[t, HI : HI + 8, :] = zeros
    for parity, ref in ((0, even_ref), (1, odd_ref)):
        for k in range(KS):
            for s in range(SL):
                rows = got_ref[pl.ds(parity * PR + k * SL + s, 16, stride=2 * PR), :]
                ref[k, PAD + 16 * s : PAD + 16 * s + 16, :] = rows * main_w[1 + s // 4]
            low = got_ref[pl.ds(parity * PR + 48 + 2 * k, 16, stride=2 * PR), :]
            high = got_ref[pl.ds(parity * PR + 49 + 2 * k, 16, stride=2 * PR), :]
            rows = jnp.where(lanes(16) < 64, roll(low, 64), high)
            ref[k, HI - 8 : HI, :] = rows[:8] * main_w[5]
            ref[k, LO : LO + 8, :] = rows[8:] * main_w[0]
        for r in range(8):
            rows = got_ref[pl.ds(parity * PR + 48 + r, 16, stride=2 * PR), :]
            ref[3, PAD + 16 * r : PAD + 16 * r + 16, :] = rows * ext_w[1 + r // 4]
            at = PAD + 128 + 16 * r
            ref[3, at : at + 16, :] = roll(rows, -18) * ext_w[3 + r // 4]
        rows = roll(got_ref[pl.ds(parity * PR + 54, 16, stride=2 * PR), :], 64)
        ref[3, HI - 8 : HI, :] = rows[:8] * ext_w[5]
        ref[3, LO : LO + 8, :] = rows[8:] * ext_w[0]
    scale = 1.0 / (48.0 * 48.0)
    for t in range(4):
        b_ref[t, 0:8, :] = zeros
        b_ref[t, HI : HI + 8, :] = zeros
        for start in range(LO, HI, 16):
            b_ref[t, start : start + 16, :] = scale * tap_rows(
                lambda at, size: even_ref[t, at : at + size, :],
                lambda at, size: odd_ref[t, at : at + size, :],
                start,
                16,
            )
    lane8 = lanes(8)
    mask_cols = jnp.zeros((8, 128), F32)
    sub8 = lax.broadcasted_iota(jnp.int32, (8, 128), 0)
    for row in range(6):
        for col in range(2):
            mask_cols = jnp.where((sub8 == row) & (lane8 == 24 + col), weights[row][col], mask_cols)
    m_ref[...] = mask_cols
    for ref, to_right in ((right_ref, True), (left_ref, False)):
        lane = lanes(72)
        packed = None
        for g in range(4):
            rows = slice(72 * g, 72 * g + 72)
            ext = b_ref[3, rows, :]
            piece = jnp.zeros((72, 128), F32)
            for k in range(KS):
                main = b_ref[k, rows, :]
                if to_right:
                    first, second = roll(main, 8 * k - 122), roll(ext, 2 * k + 5)
                    cut = 8 * k + 6
                else:
                    first, second = roll(ext, 2 * k), roll(main, 8 * k + 1)
                    cut = 8 * k + 1
                piece = jnp.where((lane >= 8 * k) & (lane < 8 * k + 8), jnp.where(lane < cut, first, second), piece)
            if g == 0:
                piece = piece + jnp.concatenate([mask_cols, jnp.zeros((64, 128), F32)], axis=0)
            piece = roll(piece, 32 * g)
            packed = piece if packed is None else packed + piece
        ref[...] = packed


def place_kernel(b_ref, out_ref):
    lane = lanes(16)
    for t in range(4):
        for start in range(0, ROWS, 16):
            rows = slice(start, start + 16)
            out = jnp.zeros((16, 128), F32)
            ext = b_ref[3, rows, :]
            if t > 0:
                off = LB + 16 * (t - 1)
                out = jnp.where(lane < off, roll(b_ref[t - 1, rows, :], off), out)
                piece = roll(ext, off - 1 - 6 * (t - 1))
                out = jnp.where((lane >= off) & (lane < off + 2), piece, out)
            if t < KS:
                off = LB + 16 * t
                out = jnp.where(lane >= off, roll(b_ref[t, rows, :], off), out)
                out = jnp.where(lane == off - 1, roll(ext, off - 1 - 6 * t), out)
                piece = roll(ext, off + 63 - (6 * t + 3))
                out = out + jnp.where((lane >= off + 63) & (lane < off + 66), piece, 0.0)
            out_ref[t, rows, :] = out


def lane_shift(parts, shift):
    rolled = [roll(part, -shift) for part in parts]
    lane = lanes(parts[0].shape[0])
    count = len(parts)
    if shift < 0:
        return [jnp.where(lane < -shift, rolled[(t - 1) % count], rolled[t]) for t in range(count)]
    return [jnp.where(lane >= 128 - shift, rolled[(t + 1) % count], rolled[t]) for t in range(count)]


def packed_columns(t):
    out = []
    for lane in range(128):
        at = 128 * t + lane
        k = min(at // LS, KS - 1)
        out.append(at - k * LS - LB)
    return out


def lane_range(lane, t, low, high):
    columns = packed_columns(t)
    where = None
    at = 0
    while at < 128:
        if low <= columns[at] < high:
            end = at
            while end < 128 and low <= columns[end] < high:
                end += 1
            piece = (lane >= at) & (lane < end)
            where = piece if where is None else where | piece
            at = end
        else:
            at += 1
    return where


def choose(where, x, y):
    return y if where is None else jnp.where(where, x, y)


def operate_kernel(
    own_ref,
    m_ref,
    from_left_ref,
    from_right_ref,
    red_ref,
    b_ref,
    p_ref,
    s_ref,
    w_ref,
    ve_ref,
    vo_ref,
    x_ref,
    ye_ref,
    yo_ref,
    t_ref,
    ve2_ref,
    vo2_ref,
    x2_ref,
    ye2_ref,
    yo2_ref,
    t2_ref,
):
    place = lax.axis_index("axial")
    inner_left = (place > 0).astype(F32)
    inner_right = (place < AN - 1).astype(F32)
    lane8 = lanes(8)
    lane16 = lanes(16)
    ones = jnp.ones((8, 128), F32)
    inside = []
    main = []
    for t in range(4):
        keep = choose(lane_range(lane8, t, -8, 0), ones * inner_left, ones)
        inside.append(choose(lane_range(lane8, t, 128, 200), ones * inner_right, keep))
        main.append(choose(lane_range(lane8, t, 0, 128), ones, jnp.zeros((8, 128), F32)))
    scale = 1.0 / (48.0**4)
    for block in range(6):

        def cell(ref, at):
            return jnp.broadcast_to(ref[block : block + 1, at : at + 1], (8, 128)) * scale

        low, high = cell(m_ref, 24), cell(m_ref, 25)
        left, right = cell(from_left_ref, 25), cell(from_right_ref, 24)
        for t in range(4):
            value = choose(lane_range(lane8, t, -8, 0), left, right)
            value = choose(lane_range(lane8, t, 0, 64), low, value)
            w_ref[t, 8 * block : 8 * block + 8, :] = choose(lane_range(lane8, t, 64, 128), high, value)

    for g in range(4):
        for start in range(72 * g, 72 * g + 72, 24):
            rows = slice(start, start + 24)
            there = slice(start - 72 * g, start - 72 * g + 24)
            lane = lanes(24)
            from_left, from_right = from_left_ref[there, :], from_right_ref[there, :]
            for t in range(4):
                out = own_ref[t, rows, :]
                if t < KS:
                    at = 2 + 16 * t
                    piece = roll(from_left, at - 8 * t - 32 * g)
                    out = out + jnp.where((lane >= at) & (lane < at + 8), piece, 0.0)
                if t > 0:
                    k = t - 1
                    at = 7 + 16 * k
                    piece = roll(from_right, at - 8 * k - 32 * g)
                    out = out + jnp.where((lane >= at) & (lane < at + 7), piece, 0.0)
                keep = jnp.concatenate([inside[t]] * 3, axis=0)
                b_ref[t, rows, :] = out * keep

    zeros = jnp.zeros((8, 128), F32)
    for t in range(4):
        for ref in (ve_ref, vo_ref, ve2_ref, vo2_ref, p_ref):
            ref[t, 0:8, :] = zeros
            ref[t, HI : HI + 8, :] = zeros
        for ref in (x_ref, x2_ref):
            for n in range(4):
                ref[n, t, 0:8, :] = zeros
                ref[n, t, HI : HI + 8, :] = zeros

    block_of = {}
    for block, (low, high) in enumerate(block_row_ranges()):
        for start in range(low, high, 8):
            block_of[start] = block

    def stages(src_ref, dst_ref, dst_shift, spread_refs, x_ref, y_refs, t_ref):
        def columns_out(start):
            rows = slice(start, start + 8)
            v = [src_ref[t, rows, :] for t in range(4)]
            before, after, second = lane_shift(v, -1), lane_shift(v, 1), lane_shift(v, 2)
            for t in range(4):
                spread_refs[0][t, rows, :] = 32.0 * v[t] + 8.0 * (before[t] + after[t])
                spread_refs[1][t, rows, :] = (before[t] + second[t]) + 23.0 * (v[t] + after[t])

        def rows_out(start):
            rows = slice(start, start + 8)
            block = block_of[start]
            for t in range(4):
                weight = w_ref[t, 8 * block : 8 * block + 8, :]
                for n, ref in enumerate(spread_refs):
                    before = ref[t, start - 1 : start + 7, :]
                    here = ref[t, rows, :]
                    after = ref[t, start + 1 : start + 9, :]
                    second = ref[t, start + 2 : start + 10, :]
                    x_ref[2 * n, t, rows, :] = (32.0 * here + 8.0 * (before + after)) * weight
                    x_ref[2 * n + 1, t, rows, :] = ((before + second) + 23.0 * (here + after)) * weight

        def rows_in(start):
            for t in range(4):
                for n, ref in enumerate(y_refs):
                    ref[t, start : start + 8, :] = tap_rows(
                        lambda at, size: x_ref[2 * n, t, at : at + size, :],
                        lambda at, size: x_ref[2 * n + 1, t, at : at + size, :],
                        start,
                        8,
                    )

        def columns_part(start):
            rows = slice(start, start + 8)
            odd = [y_refs[1][t, rows, :] for t in range(4)]
            odd_before = lane_shift(odd, -1)
            for t in range(4):
                t_ref[t, rows, :] = 8.0 * y_refs[0][t, rows, :] + 23.0 * odd[t] + odd_before[t]

        def columns_in(start):
            rows = slice(start, start + 8)
            even = [y_refs[0][t, rows, :] for t in range(4)]
            odd = [y_refs[1][t, rows, :] for t in range(4)]
            first = lane_shift([t_ref[t, rows, :] for t in range(4)], -1)
            last = lane_shift([8.0 * even[t] + odd[t] for t in range(4)], 1)
            for t in range(4):
                total = 32.0 * even[t] + 23.0 * odd[t] + first[t] + last[t]
                value = (total + ridge_weight * src_ref[t, rows, :]) * inside[t]
                dst_ref[t, start - dst_shift : start - dst_shift + 8, :] = value

        return [columns_out, rows_out, rows_in, columns_part, columns_in]

    work = [(stage, LO, HI) for stage in stages(b_ref, p_ref, 0, (ve_ref, vo_ref), x_ref, (ye_ref, yo_ref), t_ref)]
    second = stages(p_ref, s_ref, PAD, (ve2_ref, vo2_ref), x2_ref, (ye2_ref, yo2_ref), t2_ref)
    work += [(stage, LO, HI) for stage in second[:2]] + [(stage, PAD, PAD + 256) for stage in second[2:]]
    for step in range((HI - LO) // 8 + len(work) - 1):
        for n, (stage, low, high) in enumerate(work):
            start = LO + 8 * (step - n)
            if low <= start < high:
                stage(start)

    def total(x):
        return jnp.sum(jnp.sum(x, axis=0, keepdims=True), axis=1, keepdims=True)

    sums = [zeros, zeros]
    for t in range(4):
        for start in range(PAD, PAD + 256, 8):
            b = b_ref[t, start : start + 8, :] * main[t]
            p = p_ref[t, start : start + 8, :]
            sums = [sums[0] + b * b, sums[1] + b * p]
    norm, moment = total(sums[0]), total(sums[1])
    shift = jnp.where(norm > 1e-30, moment / jnp.where(norm > 1e-30, norm, 1.0), 0.0)
    shift8 = jnp.broadcast_to(shift, (8, 128))
    sums = [zeros] * 4
    for t in range(4):
        for start in range(PAD, PAD + 256, 8):
            b = b_ref[t, start : start + 8, :] * main[t]
            p = p_ref[t, start : start + 8, :] * main[t]
            s = s_ref[t, start - PAD : start - PAD + 8, :]
            w = p - shift8 * b
            z = s - shift8 * p
            sums = [sums[0] + w * b, sums[1] + w * w, sums[2] + w * z, sums[3] + b * z]
    values = [norm, moment] + [total(x) for x in sums] + [shift]
    row_lane = lax.broadcasted_iota(jnp.int32, (1, 8), 1)
    row = jnp.zeros((1, 8), F32)
    for n, value in enumerate(values):
        row = jnp.where(row_lane == n, jnp.broadcast_to(value, (1, 8)), row)
    red_ref[...] = jnp.broadcast_to(row, red_ref.shape)


def unpack_kernel(b_ref, p_ref, s_ref, bm_ref, pm_ref, sm_ref):
    for src, dst, base in ((b_ref, bm_ref, PAD), (p_ref, pm_ref, PAD), (s_ref, sm_ref, 0)):
        for k in range(KS):
            off = LB + 16 * k
            for start in range(0, 256, 16):
                first = src[k, base + start : base + start + 16, :]
                second = src[k + 1, base + start : base + start + 16, :]
                both = jnp.where(lanes(16) >= off, first, second)
                dst[k, start : start + 16, :] = roll(both, -off)


def finish_kernel(red_ref, b_ref, p_ref, s_ref, sol_hbm, res_hbm, sol_ref, res_ref, sems):
    red = red_ref[...]
    mu = red[:, 6:7]

    def total(x):
        x = jnp.sum(x, axis=0, keepdims=True)
        return [x[:, n : n + 1] for n in range(6)]

    sums = jnp.sum(red, axis=0, keepdims=True)
    norm_now, moment_all = sums[:, 0:1], sums[:, 1:2]
    step = norm_now / moment_all
    shift = mu - moment_all / norm_now
    shifted = shift * red
    _, _, _, v, wz, bz = total(red)
    _, moment_1, c_1, v_1, _, bz_1 = total(shifted)
    norm_2, moment_2 = total(shift * shifted)[:2]
    c_mu = total(mu * red)[2]
    c_mu_1 = total(mu * shifted)[2]
    norm_next = step * step * (v + 2.0 * c_1 + norm_2)
    beta = norm_next / norm_now
    r_ar = step * step * (wz + v_1 + c_mu_1 + bz_1 + moment_2)
    cross = -step * (bz + v + c_mu + 2.0 * moment_1)
    curve = r_ar + beta * cross + beta * beta * moment_all
    step_two = norm_next / curve

    def wide(x):
        return jnp.broadcast_to(x, (16, 128))

    one_beta = 1.0 + beta
    step_b, step_two_b, one_beta_b = wide(step), wide(step_two), wide(one_beta)
    copies = []
    for k in range(KS):
        for start in range(0, 256, 16):
            rows = slice(start, start + 16)
            b, p, s = b_ref[k, rows, :], p_ref[k, rows, :], s_ref[k, rows, :]
            first = step_b * p
            sol_ref[k, rows, :] = step_b * b + step_two_b * (one_beta_b * b - first)
            res_ref[k, rows, :] = (b - first) - step_two_b * (one_beta_b * p - step_b * s)
        for n, (src, dst) in enumerate(((sol_ref, sol_hbm), (res_ref, res_hbm))):
            copies.append(pltpu.make_async_copy(src.at[k], dst.at[k], sems.at[2 * k + n]))
            copies[-1].start()
    for copy in copies:
        copy.wait()


def call(kernel, outs, scratch=(), n_in=1, cost=None, hbm_in=False, hbm_out=False):
    vmem, hbm = pl.BlockSpec(memory_space=pltpu.VMEM), pl.BlockSpec(memory_space=pltpu.HBM)
    return pl.pallas_call(
        kernel,
        out_shape=[jax.ShapeDtypeStruct(shape, F32) for shape in outs],
        in_specs=[hbm if hbm_in else vmem] * n_in,
        out_specs=[hbm if hbm_out else vmem] * len(outs),
        scratch_shapes=[pltpu.VMEM(shape, F32) if isinstance(shape, tuple) else shape for shape in scratch],
        compiler_params=pltpu.CompilerParams(vmem_limit_bytes=VMEM_LIMIT),
        cost_estimate=cost,
    )


PACK_SCRATCH = [
    pltpu.VMEM((2, 4), jnp.int32),
    (KS, 1024, 128),
    (512, 128),
    (512, 128),
    pltpu.SemaphoreType.DMA((KS + 1,)),
]
FINISH_SCRATCH = [(KS, 256, 128), (KS, 256, 128), pltpu.SemaphoreType.DMA((2 * KS,))]
OPERATE_SCRATCH = [(4, 48, 128)] + 2 * ([(4, ROWS, 128)] * 2 + [(4, 4, ROWS, 128)] + [(4, ROWS, 128)] * 3)


def shards(scanned, block_mask):
    x = pltpu.with_memory_space_constraint(scanned.reshape(KS, 1024, 128), pltpu.HBM)
    mask = pltpu.with_memory_space_constraint(block_mask.T, pltpu.HBM)
    (packed,) = call(pack_kernel, [(QN * PR, 128)], PACK_SCRATCH, n_in=2, hbm_in=True)(mask, x)
    got = lax.all_to_all(packed.reshape(QN, PR, 128), "circ", 0, 0, tiled=True).reshape(QN * PR, 128)
    b_own, to_right, to_left, mask_cols = call(
        collect_kernel,
        [(4, ROWS, 128), (72, 128), (72, 128), (8, 128)],
        [(4, ROWS, 128), (4, ROWS, 128)],
    )(got)
    from_left = lax.ppermute(to_right, "axial", [(i, i + 1) for i in range(AN - 1)])
    from_right = lax.ppermute(to_left, "axial", [(i + 1, i) for i in range(AN - 1)])
    cost = pl.CostEstimate(flops=2_000_000, bytes_accessed=4_000_000, transcendentals=0)
    (own,) = call(place_kernel, [(4, ROWS, 128)], n_in=1, cost=cost)(b_own)
    red, b, p, s = call(
        operate_kernel,
        [(QN * AN, 8), (4, ROWS, 128), (4, ROWS, 128), (4, 256, 128)],
        OPERATE_SCRATCH,
        n_in=4,
    )(own, mask_cols, from_left, from_right)
    all_red = lax.all_to_all(red, ("circ", "axial"), 0, 0, tiled=True)
    bm, pm, sm = call(unpack_kernel, [(KS, 256, 128)] * 3, n_in=3, cost=cost)(b, p, s)
    return tuple(call(finish_kernel, [(KS, 256, 128)] * 2, FINISH_SCRATCH, n_in=4, hbm_out=True)(all_red, bm, pm, sm))


def solution(mesh):
    return jax.shard_map(
        shards,
        mesh=mesh,
        in_specs=(P(None, None, "circ", "axial"), P("circ", "axial")),
        out_specs=(P(None, "circ", "axial"), P(None, "circ", "axial")),
        check_vma=False,
    )
```

```python
import functools

import jax
import jax.numpy as jnp
from jax import lax
from jax.experimental import pallas as pl
from jax.experimental.pallas import tpu as pltpu
from jax.sharding import PartitionSpec as P

ridge_weight = 0.05
KS = 3
QN = 32
AN = 8
SL = 16
PR = 56
ROWS = 288
PAD = 16
LO, HI = 8, 280
LS, LB = 144, 2
SHIFT = 8
EDGE = 15
VMEM_LIMIT = 48 * 1024 * 1024
F32 = jnp.float32
BF16 = jnp.bfloat16


def column_matrix():
    sample = lax.broadcasted_iota(jnp.int32, (256, 256), 0)
    out = lax.broadcasted_iota(jnp.int32, (256, 256), 1)
    extra = out - 128
    extra = jnp.where(extra >= 18, extra - 18, extra)
    center = jnp.where(extra == 0, -2, jnp.where(extra < 3, 254 + 2 * extra, 120 + 2 * extra))
    center = jnp.where(out < 128, 2 * out, jnp.where(extra < 6, center, 1000))
    inner = (out >= 63) & (out <= 65) & (sample >= 128)
    outer = (out >= 128) & (extra >= 3) & (sample < 128)
    apart = inner | outer
    away = jnp.abs(sample - center)
    taps = jnp.where(away == 0, 32.0, jnp.where(away == 1, 23.0, jnp.where(away == 2, 8.0, 1.0)))
    return jnp.where((away > 3) | apart, 0.0, taps).astype(BF16)


def lanes(rows):
    return lax.broadcasted_iota(jnp.int32, (rows, 128), 1)


def roll(x, shift, axis=1):
    shift = shift % x.shape[axis]
    return x if shift == 0 else pltpu.roll(x, shift, axis)


def split_dot(x, matrix):
    high = x.astype(BF16)
    rest = x - high.astype(F32)
    mid = rest.astype(BF16)
    low = (rest - mid.astype(F32)).astype(BF16)
    dot = functools.partial(jnp.dot, preferred_element_type=F32)
    return dot(low, matrix) + dot(mid, matrix) + dot(high, matrix)


def pack_kernel(mask_hbm, x_hbm, out_ref, mask_ref, x_ref, main_ref, ext_ref, sems):
    q = lax.axis_index("circ")
    copies = [pltpu.make_async_copy(x_hbm.at[k], x_ref.at[k], sems.at[k]) for k in range(KS)]
    copies.append(pltpu.make_async_copy(mask_hbm, mask_ref, sems.at[KS]))
    for copy in copies:
        copy.start()
    lane = lanes(QN)
    matrix = column_matrix()
    tile = None
    ext17 = None
    next_rows = []
    for k in range(KS):
        copies[k].wait()
        left = x_ref[k, pl.ds(0, 512, stride=2), :]
        right = x_ref[k, pl.ds(1, 512, stride=2), :]
        both = split_dot(jnp.concatenate([left, right], axis=1), matrix)
        main_ref[...] = both[:, :128]
        ext_ref[...] = both[:, 128:]
        for d in range(QN):
            out_ref[pl.ds(d * PR + k * SL, SL), :] = both[d * SL : (d + 1) * SL, :128]
        ext = both[:, 128:].reshape(QN, 2, 8, 128)
        ext = jnp.where(lanes(QN * 8) < 18, ext[:, 0].reshape(QN * 8, 128), ext[:, 1].reshape(QN * 8, 128))
        ext = roll(ext, 6 * k)
        tile = ext if tile is None else tile + ext

        def neighbour(ref):
            first = ref[pl.ds(0, QN, stride=SL), :]
            last = ref[pl.ds(SL - 1, QN, stride=SL), :]
            return jnp.where(q >= QN // 2, roll(last, 1, 0), roll(first, -1, 0))

        next_rows.append(neighbour(main_ref))
        ext_row = roll(jnp.where(lane < 6, neighbour(ext_ref), 0.0), 6 * k)
        ext17 = ext_row if ext17 is None else ext17 + ext_row
    for d in range(QN):
        out_ref[pl.ds(d * PR + 48, 8), :] = tile[d * 8 : (d + 1) * 8]
    copies[KS].wait()
    mask = mask_ref[...].astype(F32)
    mask_row = jnp.zeros((1, 128), F32)
    for row in range(4):
        for col in range(2):
            value = jnp.broadcast_to(mask[col : col + 1, row : row + 1], (1, 128))
            mask_row = jnp.where(lanes(1) == 64 + 2 * row + col, value, mask_row)
    mask_row = jnp.broadcast_to(mask_row, (QN, 128))
    fill = []
    for k in range(KS):
        fill += [roll(next_rows[k], 64), next_rows[k]]
    fill += [roll(ext17, 64), mask_row]
    for row in range(8):
        where = pl.ds(48 + row, QN, stride=PR)
        out_ref[where, :] = jnp.where(lane < 64, out_ref[where, :], fill[row])


def tap_rows(even, odd, start, size):
    def ev(offset):
        return even(start + offset, size)

    def od(offset):
        return odd(start + offset, size)

    return (
        32.0 * ev(0) + 8.0 * (ev(-1) + ev(1)) + 23.0 * (od(-1) + od(0)) + (od(-2) + od(1))
    )


def block_row_ranges():
    edges = [LO] + [PAD + 64 * b for b in range(5)] + [HI]
    return list(zip(edges[:-1], edges[1:]))


def collect_kernel(got_ref, b_ref, left_ref, m_ref, even_ref, odd_ref):
    d = lax.axis_index("circ")
    row_lane = lanes(1)

    def spread_lane(x, at):
        return jnp.broadcast_to(x[:, at : at + 1], (1, 128))

    before = got_ref[pl.ds(lax.rem(d + QN - 1, QN) * PR + 55, 1), :]
    after = got_ref[pl.ds(lax.rem(d + 1, QN) * PR + 55, 1), :]
    weights = [(spread_lane(before, 70), spread_lane(before, 71))]
    mine = got_ref[pl.ds(d * PR + 55, 1), :]
    for row in range(4):
        weights.append(tuple(spread_lane(mine, 64 + 2 * row + col) for col in range(2)))
    weights.append((spread_lane(after, 64), spread_lane(after, 65)))
    main_w = [jnp.where(row_lane <= 65, low, high) for low, high in weights]
    ext_first = (row_lane == 0) | (row_lane == 6) | (row_lane == 12)
    ext_w = [jnp.where(ext_first, low, high) for low, high in weights]
    zeros = jnp.zeros((8, 128), F32)
    for ref in (even_ref, odd_ref):
        for t in range(4):
            ref[t, 0:8, :] = zeros
            ref[t, HI : HI + 8, :] = zeros
    for parity, ref in ((0, even_ref), (1, odd_ref)):
        for k in range(KS):
            for s in range(SL):
                rows = got_ref[pl.ds(parity * PR + k * SL + s, 16, stride=2 * PR), :]
                ref[k, PAD + 16 * s : PAD + 16 * s + 16, :] = rows * main_w[1 + s // 4]
            low = got_ref[pl.ds(parity * PR + 48 + 2 * k, 16, stride=2 * PR), :]
            high = got_ref[pl.ds(parity * PR + 49 + 2 * k, 16, stride=2 * PR), :]
            rows = jnp.where(lanes(16) < 64, roll(low, 64), high)
            ref[k, HI - 8 : HI, :] = rows[:8] * main_w[5]
            ref[k, LO : LO + 8, :] = rows[8:] * main_w[0]
        for r in range(8):
            rows = got_ref[pl.ds(parity * PR + 48 + r, 16, stride=2 * PR), :]
            ref[3, PAD + 16 * r : PAD + 16 * r + 16, :] = rows * ext_w[1 + r // 4]
            at = PAD + 128 + 16 * r
            ref[3, at : at + 16, :] = roll(rows, -18) * ext_w[3 + r // 4]
        rows = roll(got_ref[pl.ds(parity * PR + 54, 16, stride=2 * PR), :], 64)
        ref[3, HI - 8 : HI, :] = rows[:8] * ext_w[5]
        ref[3, LO : LO + 8, :] = rows[8:] * ext_w[0]
    scale = 1.0 / (48.0 * 48.0)
    for t in range(4):
        b_ref[t, 0:8, :] = zeros
        b_ref[t, HI : HI + 8, :] = zeros
        for start in range(LO, HI, 16):
            b_ref[t, start : start + 16, :] = scale * tap_rows(
                lambda at, size: even_ref[t, at : at + size, :],
                lambda at, size: odd_ref[t, at : at + size, :],
                start,
                16,
            )
    lane8 = lanes(8)
    mask_cols = jnp.zeros((8, 128), F32)
    sub8 = lax.broadcasted_iota(jnp.int32, (8, 128), 0)
    for row in range(6):
        for col in range(2):
            mask_cols = jnp.where((sub8 == row) & (lane8 == 24 + col), weights[row][col], mask_cols)
    m_ref[...] = mask_cols
    first_col = jnp.zeros((8, 128), F32)
    for row in range(6):
        first_col = jnp.where((sub8 == row) & (lane8 == EDGE), weights[row][0], first_col)
    lane16 = lanes(16)
    for start in range(0, ROWS // 2, 16):
        halves = []
        for g in range(2):
            rows = slice(start + g * ROWS // 2, start + g * ROWS // 2 + 16)
            ext = b_ref[3, rows, :]
            piece = jnp.zeros((16, 128), F32)
            for k in range(KS):
                at = 16 * k
                piece = jnp.where(lane16 == at, roll(ext, at - 6 * k), piece)
                piece = jnp.where((lane16 > at) & (lane16 < at + EDGE), roll(b_ref[k, rows, :], at + 1), piece)
            halves.append(piece)
        out = halves[0] + roll(halves[1], 64)
        if start == 0:
            out = out + jnp.concatenate([first_col, zeros], axis=0)
        left_ref[start : start + 16, :] = out


def place_kernel(b_ref, out_ref):
    lane = lanes(16)
    for t in range(4):
        for start in range(0, ROWS, 16):
            rows = slice(start, start + 16)
            out = jnp.zeros((16, 128), F32)
            ext = b_ref[3, rows, :]
            if t > 0:
                off = LB + 16 * (t - 1)
                out = jnp.where(lane < off, roll(b_ref[t - 1, rows, :], off), out)
                piece = roll(ext, off - 1 - 6 * (t - 1))
                out = jnp.where((lane >= off) & (lane < off + 2), piece, out)
            if t < KS:
                off = LB + 16 * t
                out = jnp.where(lane >= off, roll(b_ref[t, rows, :], off), out)
                piece = roll(ext, off + 63 - (6 * t + 3))
                out = out + jnp.where((lane >= off + 63) & (lane < off + 66), piece, 0.0)
            out_ref[t, rows, :] = out


def lane_shift(parts, shift):
    rolled = [roll(part, -shift) for part in parts]
    lane = lanes(parts[0].shape[0])
    count = len(parts)
    if shift < 0:
        return [jnp.where(lane < -shift, rolled[(t - 1) % count], rolled[t]) for t in range(count)]
    return [jnp.where(lane >= 128 - shift, rolled[(t + 1) % count], rolled[t]) for t in range(count)]


def packed_columns(t):
    out = []
    for lane in range(128):
        at = 128 * t + lane
        k = min(at // LS, KS - 1)
        out.append(at - k * LS - LB)
    return out


def lane_range(lane, t, low, high):
    columns = packed_columns(t)
    where = None
    at = 0
    while at < 128:
        if low <= columns[at] < high:
            end = at
            while end < 128 and low <= columns[end] < high:
                end += 1
            piece = (lane >= at) & (lane < end)
            where = piece if where is None else where | piece
            at = end
        else:
            at += 1
    return where


def choose(where, x, y):
    return y if where is None else jnp.where(where, x, y)


def operate_kernel(
    own_ref,
    m_ref,
    from_right_ref,
    red_ref,
    b_ref,
    p_ref,
    s_ref,
    w_ref,
    ve_ref,
    vo_ref,
    x_ref,
    ye_ref,
    yo_ref,
    t_ref,
    ve2_ref,
    vo2_ref,
    x2_ref,
    ye2_ref,
    yo2_ref,
    t2_ref,
):
    place = lax.axis_index("axial")
    first_tile = (place == 0).astype(F32)
    inner_right = (place < AN - 1).astype(F32)
    lane8 = lanes(8)
    lane16 = lanes(16)
    ones = jnp.ones((8, 128), F32)
    inside = []
    main = []
    for t in range(4):
        keep = choose(lane_range(lane8, t, -LB, 0), jnp.zeros((8, 128), F32), ones)
        inside.append(choose(lane_range(lane8, t, 128, 400), ones * inner_right, keep))
        own = choose(lane_range(lane8, t, SHIFT, SHIFT + 128), ones, jnp.zeros((8, 128), F32))
        main.append(choose(lane_range(lane8, t, 0, SHIFT), ones * first_tile, own))
    scale = 1.0 / (48.0**4)
    for block in range(6):

        def cell(ref, at):
            return jnp.broadcast_to(ref[block : block + 1, at : at + 1], (8, 128)) * scale

        low, high = cell(m_ref, 24), cell(m_ref, 25)
        right = cell(from_right_ref, EDGE)
        for t in range(4):
            value = choose(lane_range(lane8, t, -LB, 0), jnp.zeros((8, 128), F32), right)
            value = choose(lane_range(lane8, t, 0, 64), low, value)
            w_ref[t, 8 * block : 8 * block + 8, :] = choose(lane_range(lane8, t, 64, 128), high, value)

    for g in range(2):
        for there in range(0, ROWS // 2, 16):
            rows = slice(there + g * ROWS // 2, there + g * ROWS // 2 + 16)
            piece = roll(from_right_ref[there : there + 16, :], LB - 1 - 64 * g)
            for t in range(4):
                out = own_ref[t, rows, :]
                if t > 0:
                    at = LB - 1 + 16 * (t - 1)
                    out = out + jnp.where((lane16 >= at) & (lane16 < at + EDGE), piece, 0.0)
                b_ref[t, rows, :] = out * jnp.concatenate([inside[t]] * 2, axis=0)

    zeros = jnp.zeros((8, 128), F32)
    for t in range(4):
        for ref in (ve_ref, vo_ref, ve2_ref, vo2_ref, p_ref):
            ref[t, 0:8, :] = zeros
            ref[t, HI : HI + 8, :] = zeros
        for ref in (x_ref, x2_ref):
            for n in range(4):
                ref[n, t, 0:8, :] = zeros
                ref[n, t, HI : HI + 8, :] = zeros

    block_of = {}
    for block, (low, high) in enumerate(block_row_ranges()):
        for start in range(low, high, 8):
            block_of[start] = block

    def stages(src_ref, dst_ref, dst_shift, spread_refs, x_ref, y_refs, t_ref):
        def columns_out(start):
            rows = slice(start, start + 8)
            v = [src_ref[t, rows, :] for t in range(4)]
            before, after, second = lane_shift(v, -1), lane_shift(v, 1), lane_shift(v, 2)
            for t in range(4):
                spread_refs[0][t, rows, :] = 32.0 * v[t] + 8.0 * (before[t] + after[t])
                spread_refs[1][t, rows, :] = (before[t] + second[t]) + 23.0 * (v[t] + after[t])

        def rows_out(start):
            rows = slice(start, start + 8)
            block = block_of[start]
            for t in range(4):
                weight = w_ref[t, 8 * block : 8 * block + 8, :]
                for n, ref in enumerate(spread_refs):
                    before = ref[t, start - 1 : start + 7, :]
                    here = ref[t, rows, :]
                    after = ref[t, start + 1 : start + 9, :]
                    second = ref[t, start + 2 : start + 10, :]
                    x_ref[2 * n, t, rows, :] = (32.0 * here + 8.0 * (before + after)) * weight
                    x_ref[2 * n + 1, t, rows, :] = ((before + second) + 23.0 * (here + after)) * weight

        def rows_in(start):
            for t in range(4):
                for n, ref in enumerate(y_refs):
                    ref[t, start : start + 8, :] = tap_rows(
                        lambda at, size: x_ref[2 * n, t, at : at + size, :],
                        lambda at, size: x_ref[2 * n + 1, t, at : at + size, :],
                        start,
                        8,
                    )

        def columns_part(start):
            rows = slice(start, start + 8)
            odd = [y_refs[1][t, rows, :] for t in range(4)]
            odd_before = lane_shift(odd, -1)
            for t in range(4):
                t_ref[t, rows, :] = 8.0 * y_refs[0][t, rows, :] + 23.0 * odd[t] + odd_before[t]

        def columns_in(start):
            rows = slice(start, start + 8)
            even = [y_refs[0][t, rows, :] for t in range(4)]
            odd = [y_refs[1][t, rows, :] for t in range(4)]
            first = lane_shift([t_ref[t, rows, :] for t in range(4)], -1)
            last = lane_shift([8.0 * even[t] + odd[t] for t in range(4)], 1)
            for t in range(4):
                total = 32.0 * even[t] + 23.0 * odd[t] + first[t] + last[t]
                value = (total + ridge_weight * src_ref[t, rows, :]) * inside[t]
                dst_ref[t, start - dst_shift : start - dst_shift + 8, :] = value

        return [columns_out, rows_out, rows_in, columns_part, columns_in]

    work = [(stage, LO, HI) for stage in stages(b_ref, p_ref, 0, (ve_ref, vo_ref), x_ref, (ye_ref, yo_ref), t_ref)]
    second = stages(p_ref, s_ref, PAD, (ve2_ref, vo2_ref), x2_ref, (ye2_ref, yo2_ref), t2_ref)
    work += [(stage, LO, HI) for stage in second[:2]] + [(stage, PAD, PAD + 256) for stage in second[2:]]
    for step in range((HI - LO) // 8 + len(work) - 1):
        for n, (stage, low, high) in enumerate(work):
            start = LO + 8 * (step - n)
            if low <= start < high:
                stage(start)

    def total(x):
        return jnp.sum(jnp.sum(x, axis=0, keepdims=True), axis=1, keepdims=True)

    sums = [zeros, zeros]
    for t in range(4):
        for start in range(PAD, PAD + 256, 8):
            b = b_ref[t, start : start + 8, :] * main[t]
            p = p_ref[t, start : start + 8, :]
            sums = [sums[0] + b * b, sums[1] + b * p]
    norm, moment = total(sums[0]), total(sums[1])
    shift = jnp.where(norm > 1e-30, moment / jnp.where(norm > 1e-30, norm, 1.0), 0.0)
    shift8 = jnp.broadcast_to(shift, (8, 128))
    sums = [zeros] * 4
    for t in range(4):
        for start in range(PAD, PAD + 256, 8):
            b = b_ref[t, start : start + 8, :] * main[t]
            p = p_ref[t, start : start + 8, :] * main[t]
            s = s_ref[t, start - PAD : start - PAD + 8, :]
            w = p - shift8 * b
            z = s - shift8 * p
            sums = [sums[0] + w * b, sums[1] + w * w, sums[2] + w * z, sums[3] + b * z]
    values = [norm, moment] + [total(x) for x in sums] + [shift]
    row_lane = lax.broadcasted_iota(jnp.int32, (1, 8), 1)
    row = jnp.zeros((1, 8), F32)
    for n, value in enumerate(values):
        row = jnp.where(row_lane == n, jnp.broadcast_to(value, (1, 8)), row)
    red_ref[...] = jnp.broadcast_to(row, red_ref.shape)


def edges_kernel(b_ref, p_ref, s_ref, out_ref):
    lane = lanes(16)
    for start in range(0, 256, 16):
        out = jnp.zeros((16, 128), F32)
        for n, (src, base) in enumerate(((b_ref, PAD), (p_ref, PAD), (s_ref, 0))):
            for k in range(KS):
                at = SHIFT * (KS * n + k)
                piece = roll(src[k + 1, base + start : base + start + 16, :], at - (LB + 16 * k))
                out = jnp.where((lane >= at) & (lane < at + SHIFT), piece, out)
        out_ref[start : start + 16, :] = out


def unpack_kernel(b_ref, p_ref, s_ref, edge_ref, bm_ref, pm_ref, sm_ref):
    first_tile = lax.axis_index("axial") == 0
    lane = lanes(16)
    own = (lane >= SHIFT) | first_tile
    for n, (src, dst, base) in enumerate(((b_ref, bm_ref, PAD), (p_ref, pm_ref, PAD), (s_ref, sm_ref, 0))):
        for k in range(KS):
            off = LB + 16 * k
            for start in range(0, 256, 16):
                first = src[k, base + start : base + start + 16, :]
                second = src[k + 1, base + start : base + start + 16, :]
                both = roll(jnp.where(lane >= off, first, second), -off)
                edge = roll(edge_ref[start : start + 16, :], -SHIFT * (KS * n + k))
                dst[k, start : start + 16, :] = jnp.where(own, both, edge)


def finish_kernel(red_ref, b_ref, p_ref, s_ref, sol_hbm, res_hbm, sol_ref, res_ref, sems):
    red = red_ref[...]
    mu = red[:, 6:7]

    def total(x):
        x = jnp.sum(x, axis=0, keepdims=True)
        return [x[:, n : n + 1] for n in range(6)]

    sums = jnp.sum(red, axis=0, keepdims=True)
    norm_now, moment_all = sums[:, 0:1], sums[:, 1:2]
    step = norm_now / moment_all
    shift = mu - moment_all / norm_now
    shifted = shift * red
    _, _, _, v, wz, bz = total(red)
    _, moment_1, c_1, v_1, _, bz_1 = total(shifted)
    norm_2, moment_2 = total(shift * shifted)[:2]
    c_mu = total(mu * red)[2]
    c_mu_1 = total(mu * shifted)[2]
    norm_next = step * step * (v + 2.0 * c_1 + norm_2)
    beta = norm_next / norm_now
    r_ar = step * step * (wz + v_1 + c_mu_1 + bz_1 + moment_2)
    cross = -step * (bz + v + c_mu + 2.0 * moment_1)
    curve = r_ar + beta * cross + beta * beta * moment_all
    step_two = norm_next / curve

    def wide(x):
        return jnp.broadcast_to(x, (16, 128))

    one_beta = 1.0 + beta
    step_b, step_two_b, one_beta_b = wide(step), wide(step_two), wide(one_beta)
    copies = []
    for k in range(KS):
        for start in range(0, 256, 16):
            rows = slice(start, start + 16)
            b, p, s = b_ref[k, rows, :], p_ref[k, rows, :], s_ref[k, rows, :]
            first = step_b * p
            sol_ref[k, rows, :] = step_b * b + step_two_b * (one_beta_b * b - first)
            res_ref[k, rows, :] = (b - first) - step_two_b * (one_beta_b * p - step_b * s)
        for n, (src, dst) in enumerate(((sol_ref, sol_hbm), (res_ref, res_hbm))):
            copies.append(pltpu.make_async_copy(src.at[k], dst.at[k], sems.at[2 * k + n]))
            copies[-1].start()
    for copy in copies:
        copy.wait()


def call(kernel, outs, scratch=(), n_in=1, cost=None, hbm_in=False, hbm_out=False):
    vmem, hbm = pl.BlockSpec(memory_space=pltpu.VMEM), pl.BlockSpec(memory_space=pltpu.HBM)
    return pl.pallas_call(
        kernel,
        out_shape=[jax.ShapeDtypeStruct(shape, F32) for shape in outs],
        in_specs=[hbm if hbm_in else vmem] * n_in,
        out_specs=[hbm if hbm_out else vmem] * len(outs),
        scratch_shapes=[pltpu.VMEM(shape, F32) if isinstance(shape, tuple) else shape for shape in scratch],
        compiler_params=pltpu.CompilerParams(vmem_limit_bytes=VMEM_LIMIT),
        cost_estimate=cost,
    )


PACK_SCRATCH = [
    pltpu.VMEM((2, 4), jnp.int32),
    (KS, 1024, 128),
    (512, 128),
    (512, 128),
    pltpu.SemaphoreType.DMA((KS + 1,)),
]
FINISH_SCRATCH = [(KS, 256, 128), (KS, 256, 128), pltpu.SemaphoreType.DMA((2 * KS,))]
OPERATE_SCRATCH = [(4, 48, 128)] + 2 * ([(4, ROWS, 128)] * 2 + [(4, 4, ROWS, 128)] + [(4, ROWS, 128)] * 3)


def shards(scanned, block_mask):
    x = pltpu.with_memory_space_constraint(scanned.reshape(KS, 1024, 128), pltpu.HBM)
    mask = pltpu.with_memory_space_constraint(block_mask.T, pltpu.HBM)
    (packed,) = call(pack_kernel, [(QN * PR, 128)], PACK_SCRATCH, n_in=2, hbm_in=True)(mask, x)
    got = lax.all_to_all(packed.reshape(QN, PR, 128), "circ", 0, 0, tiled=True).reshape(QN * PR, 128)
    b_own, to_left, mask_cols = call(
        collect_kernel,
        [(4, ROWS, 128), (ROWS // 2, 128), (8, 128)],
        [(4, ROWS, 128), (4, ROWS, 128)],
    )(got)
    from_right = lax.ppermute(to_left, "axial", [(i + 1, i) for i in range(AN - 1)])
    cost = pl.CostEstimate(flops=2_000_000, bytes_accessed=4_000_000, transcendentals=0)
    (own,) = call(place_kernel, [(4, ROWS, 128)], n_in=1, cost=cost)(b_own)
    red, b, p, s = call(
        operate_kernel,
        [(QN * AN, 8), (4, ROWS, 128), (4, ROWS, 128), (4, 256, 128)],
        OPERATE_SCRATCH,
        n_in=3,
    )(own, mask_cols, from_right)
    all_red = lax.all_to_all(red, ("circ", "axial"), 0, 0, tiled=True)

    def share(b, p, s):
        (edges,) = call(edges_kernel, [(256, 128)], n_in=3, cost=cost)(b, p, s)
        edge = lax.ppermute(edges, "axial", [(i, i + 1) for i in range(AN - 1)])
        return tuple(call(unpack_kernel, [(KS, 256, 128)] * 3, n_in=4, cost=cost)(b, p, s, edge))

    def keep(b, p, s):
        return tuple(x[:KS, :256] for x in (b, p, s))

    bm, pm, sm = lax.cond(block_mask[0, 0] < 2, share, keep, b, p, s)
    return tuple(call(finish_kernel, [(KS, 256, 128)] * 2, FINISH_SCRATCH, n_in=4, hbm_out=True)(all_red, bm, pm, sm))


def solution(mesh):
    return jax.shard_map(
        shards,
        mesh=mesh,
        in_specs=(P(None, None, "circ", "axial"), P("circ", "axial")),
        out_specs=(P(None, "circ", "axial"), P(None, "circ", "axial")),
        check_vma=False,
    )
```

```python
import functools

import jax
import jax.numpy as jnp
from jax import lax
from jax.experimental import pallas as pl
from jax.experimental.pallas import tpu as pltpu
from jax.sharding import PartitionSpec as P

ridge_weight = 0.05
KS = 3
QN = 32
AN = 8
SL = 16
PR = 56
ROWS = 288
PAD = 16
LO, HI = 8, 280
LS, LB = 144, 2
SHIFT = 8
EDGE = 15
VMEM_LIMIT = 48 * 1024 * 1024
F32 = jnp.float32
BF16 = jnp.bfloat16


def column_matrix():
    sample = lax.broadcasted_iota(jnp.int32, (256, 256), 0)
    out = lax.broadcasted_iota(jnp.int32, (256, 256), 1)
    extra = out - 128
    extra = jnp.where(extra >= 18, extra - 18, extra)
    center = jnp.where(extra == 0, -2, jnp.where(extra < 3, 254 + 2 * extra, 120 + 2 * extra))
    center = jnp.where(out < 128, 2 * out, jnp.where(extra < 6, center, 1000))
    inner = (out >= 63) & (out <= 65) & (sample >= 128)
    outer = (out >= 128) & (extra >= 3) & (sample < 128)
    apart = inner | outer
    away = jnp.abs(sample - center)
    taps = jnp.where(away == 0, 32.0, jnp.where(away == 1, 23.0, jnp.where(away == 2, 8.0, 1.0)))
    return jnp.where((away > 3) | apart, 0.0, taps).astype(BF16)


def lanes(rows):
    return lax.broadcasted_iota(jnp.int32, (rows, 128), 1)


def roll(x, shift, axis=1):
    shift = shift % x.shape[axis]
    return x if shift == 0 else pltpu.roll(x, shift, axis)


def split_dot(x, matrix):
    high = x.astype(BF16)
    rest = x - high.astype(F32)
    mid = rest.astype(BF16)
    low = (rest - mid.astype(F32)).astype(BF16)
    dot = functools.partial(jnp.dot, preferred_element_type=F32)
    return dot(low, matrix) + dot(mid, matrix) + dot(high, matrix)


def pack_kernel(mask_hbm, x_hbm, out_ref, mask_ref, x_ref, main_ref, ext_ref, sems):
    q = lax.axis_index("circ")
    copies = [pltpu.make_async_copy(x_hbm.at[k], x_ref.at[k], sems.at[k]) for k in range(KS)]
    copies.append(pltpu.make_async_copy(mask_hbm, mask_ref, sems.at[KS]))
    for copy in copies:
        copy.start()
    lane = lanes(QN)
    matrix = column_matrix()
    tile = None
    ext17 = None
    next_rows = []
    for k in range(KS):
        copies[k].wait()
        left = x_ref[k, pl.ds(0, 512, stride=2), :]
        right = x_ref[k, pl.ds(1, 512, stride=2), :]
        both = split_dot(jnp.concatenate([left, right], axis=1), matrix)
        main_ref[...] = both[:, :128]
        ext_ref[...] = both[:, 128:]
        for d in range(QN):
            out_ref[pl.ds(d * PR + k * SL, SL), :] = both[d * SL : (d + 1) * SL, :128]
        ext = both[:, 128:].reshape(QN, 2, 8, 128)
        ext = jnp.where(lanes(QN * 8) < 18, ext[:, 0].reshape(QN * 8, 128), ext[:, 1].reshape(QN * 8, 128))
        ext = roll(ext, 6 * k)
        tile = ext if tile is None else tile + ext

        def neighbour(ref):
            first = ref[pl.ds(0, QN, stride=SL), :]
            last = ref[pl.ds(SL - 1, QN, stride=SL), :]
            return jnp.where(q >= QN // 2, roll(last, 1, 0), roll(first, -1, 0))

        next_rows.append(neighbour(main_ref))
        ext_row = roll(jnp.where(lane < 6, neighbour(ext_ref), 0.0), 6 * k)
        ext17 = ext_row if ext17 is None else ext17 + ext_row
    for d in range(QN):
        out_ref[pl.ds(d * PR + 48, 8), :] = tile[d * 8 : (d + 1) * 8]
    copies[KS].wait()
    mask = mask_ref[...].astype(F32)
    mask_row = jnp.zeros((1, 128), F32)
    for row in range(4):
        for col in range(2):
            value = jnp.broadcast_to(mask[col : col + 1, row : row + 1], (1, 128))
            mask_row = jnp.where(lanes(1) == 64 + 2 * row + col, value, mask_row)
    mask_row = jnp.broadcast_to(mask_row, (QN, 128))
    fill = []
    for k in range(KS):
        fill += [roll(next_rows[k], 64), next_rows[k]]
    fill += [roll(ext17, 64), mask_row]
    for row in range(8):
        where = pl.ds(48 + row, QN, stride=PR)
        out_ref[where, :] = jnp.where(lane < 64, out_ref[where, :], fill[row])


def tap_rows(even, odd, start, size):
    def ev(offset):
        return even(start + offset, size)

    def od(offset):
        return odd(start + offset, size)

    return (
        4.0 * ev(0) + (ev(-1) + ev(1)) + 23.0 * (od(-1) + od(0)) + (od(-2) + od(1))
    )


def block_row_ranges():
    edges = [LO] + [PAD + 64 * b for b in range(5)] + [HI]
    return list(zip(edges[:-1], edges[1:]))


def collect_kernel(got_ref, b_ref, left_ref, m_ref, even_ref, odd_ref):
    d = lax.axis_index("circ")
    row_lane = lanes(1)

    def spread_lane(x, at):
        return jnp.broadcast_to(x[:, at : at + 1], (1, 128))

    before = got_ref[pl.ds(lax.rem(d + QN - 1, QN) * PR + 55, 1), :]
    after = got_ref[pl.ds(lax.rem(d + 1, QN) * PR + 55, 1), :]
    weights = [(spread_lane(before, 70), spread_lane(before, 71))]
    mine = got_ref[pl.ds(d * PR + 55, 1), :]
    for row in range(4):
        weights.append(tuple(spread_lane(mine, 64 + 2 * row + col) for col in range(2)))
    weights.append((spread_lane(after, 64), spread_lane(after, 65)))
    all_main_w = [jnp.where(row_lane <= 65, low, high) for low, high in weights]
    ext_first = (row_lane == 0) | (row_lane == 6) | (row_lane == 12)
    all_ext_w = [jnp.where(ext_first, low, high) for low, high in weights]
    zeros = jnp.zeros((8, 128), F32)
    for ref in (even_ref, odd_ref):
        for t in range(4):
            ref[t, 0:8, :] = zeros
            ref[t, HI : HI + 8, :] = zeros
    for parity, ref in ((0, even_ref), (1, odd_ref)):
        if parity == 0:
            main_w, ext_w = [8.0 * w for w in all_main_w], [8.0 * w for w in all_ext_w]
        else:
            main_w, ext_w = all_main_w, all_ext_w
        for k in range(KS):
            for s in range(SL):
                rows = got_ref[pl.ds(parity * PR + k * SL + s, 16, stride=2 * PR), :]
                ref[k, PAD + 16 * s : PAD + 16 * s + 16, :] = rows * main_w[1 + s // 4]
            low = got_ref[pl.ds(parity * PR + 48 + 2 * k, 16, stride=2 * PR), :]
            high = got_ref[pl.ds(parity * PR + 49 + 2 * k, 16, stride=2 * PR), :]
            rows = jnp.where(lanes(16) < 64, roll(low, 64), high)
            ref[k, HI - 8 : HI, :] = rows[:8] * main_w[5]
            ref[k, LO : LO + 8, :] = rows[8:] * main_w[0]
        for r in range(8):
            rows = got_ref[pl.ds(parity * PR + 48 + r, 16, stride=2 * PR), :]
            ref[3, PAD + 16 * r : PAD + 16 * r + 16, :] = rows * ext_w[1 + r // 4]
            at = PAD + 128 + 16 * r
            ref[3, at : at + 16, :] = roll(rows, -18) * ext_w[3 + r // 4]
        rows = roll(got_ref[pl.ds(parity * PR + 54, 16, stride=2 * PR), :], 64)
        ref[3, HI - 8 : HI, :] = rows[:8] * ext_w[5]
        ref[3, LO : LO + 8, :] = rows[8:] * ext_w[0]
    scale = 1.0 / (48.0 * 48.0)
    for t in range(4):
        b_ref[t, 0:8, :] = zeros
        b_ref[t, HI : HI + 8, :] = zeros
        for start in range(LO, HI, 16):
            b_ref[t, start : start + 16, :] = scale * tap_rows(
                lambda at, size: even_ref[t, at : at + size, :],
                lambda at, size: odd_ref[t, at : at + size, :],
                start,
                16,
            )
    lane8 = lanes(8)
    mask_cols = jnp.zeros((8, 128), F32)
    sub8 = lax.broadcasted_iota(jnp.int32, (8, 128), 0)
    for row in range(6):
        for col in range(2):
            mask_cols = jnp.where((sub8 == row) & (lane8 == 24 + col), weights[row][col], mask_cols)
    m_ref[...] = mask_cols
    first_col = jnp.zeros((8, 128), F32)
    for row in range(6):
        first_col = jnp.where((sub8 == row) & (lane8 == EDGE), weights[row][0], first_col)
    lane16 = lanes(16)
    for start in range(0, ROWS // 2, 16):
        halves = []
        for g in range(2):
            rows = slice(start + g * ROWS // 2, start + g * ROWS // 2 + 16)
            ext = b_ref[3, rows, :]
            piece = jnp.zeros((16, 128), F32)
            for k in range(KS):
                at = 16 * k
                piece = jnp.where(lane16 == at, roll(ext, at - 6 * k), piece)
                piece = jnp.where((lane16 > at) & (lane16 < at + EDGE), roll(b_ref[k, rows, :], at + 1), piece)
            halves.append(piece)
        out = halves[0] + roll(halves[1], 64)
        if start == 0:
            out = out + jnp.concatenate([first_col, zeros], axis=0)
        left_ref[start : start + 16, :] = out


def place_kernel(b_ref, out_ref, flag_ref):
    flag_ref[0] = 1
    lane = lanes(16)
    for t in range(4):
        for start in range(0, ROWS, 16):
            rows = slice(start, start + 16)
            out = jnp.zeros((16, 128), F32)
            ext = b_ref[3, rows, :]
            if t > 0:
                off = LB + 16 * (t - 1)
                out = jnp.where(lane < off, roll(b_ref[t - 1, rows, :], off), out)
                piece = roll(ext, off - 1 - 6 * (t - 1))
                out = jnp.where((lane >= off) & (lane < off + 2), piece, out)
            if t < KS:
                off = LB + 16 * t
                out = jnp.where(lane >= off, roll(b_ref[t, rows, :], off), out)
                piece = roll(ext, off + 63 - (6 * t + 3))
                out = out + jnp.where((lane >= off + 63) & (lane < off + 66), piece, 0.0)
            out_ref[t, rows, :] = out


def lane_shift(parts, shift):
    rolled = [roll(part, -shift) for part in parts]
    lane = lanes(parts[0].shape[0])
    count = len(parts)
    if shift < 0:
        return [jnp.where(lane < -shift, rolled[(t - 1) % count], rolled[t]) for t in range(count)]
    return [jnp.where(lane >= 128 - shift, rolled[(t + 1) % count], rolled[t]) for t in range(count)]


def packed_columns(t):
    out = []
    for lane in range(128):
        at = 128 * t + lane
        k = min(at // LS, KS - 1)
        out.append(at - k * LS - LB)
    return out


def lane_range(lane, t, low, high):
    columns = packed_columns(t)
    where = None
    at = 0
    while at < 128:
        if low <= columns[at] < high:
            end = at
            while end < 128 and low <= columns[end] < high:
                end += 1
            piece = (lane >= at) & (lane < end)
            where = piece if where is None else where | piece
            at = end
        else:
            at += 1
    return where


def choose(where, x, y):
    return y if where is None else jnp.where(where, x, y)


def operate_kernel(
    own_ref,
    m_ref,
    from_right_ref,
    red_ref,
    b_ref,
    p_ref,
    s_ref,
    w_ref,
    ve_ref,
    vo_ref,
    x_ref,
    ye_ref,
    yo_ref,
    t_ref,
    ve2_ref,
    vo2_ref,
    x2_ref,
    ye2_ref,
    yo2_ref,
    t2_ref,
):
    place = lax.axis_index("axial")
    first_tile = (place == 0).astype(F32)
    inner_right = (place < AN - 1).astype(F32)
    lane8 = lanes(8)
    lane16 = lanes(16)
    ones = jnp.ones((8, 128), F32)
    inside = []
    main = []
    for t in range(4):
        keep = choose(lane_range(lane8, t, -LB, 0), jnp.zeros((8, 128), F32), ones)
        inside.append(choose(lane_range(lane8, t, 128, 400), ones * inner_right, keep))
        own = choose(lane_range(lane8, t, SHIFT, SHIFT + 128), ones, jnp.zeros((8, 128), F32))
        main.append(choose(lane_range(lane8, t, 0, SHIFT), ones * first_tile, own))
    scale = 1.0 / (48.0**4)
    for block in range(6):

        def cell(ref, at):
            return jnp.broadcast_to(ref[block : block + 1, at : at + 1], (8, 128)) * scale

        low, high = cell(m_ref, 24), cell(m_ref, 25)
        right = cell(from_right_ref, EDGE)
        for t in range(4):
            value = choose(lane_range(lane8, t, -LB, 0), jnp.zeros((8, 128), F32), right)
            value = choose(lane_range(lane8, t, 0, 64), low, value)
            value = choose(lane_range(lane8, t, 64, 128), high, value)
            for power in range(3):
                w_ref[power, t, 8 * block : 8 * block + 8, :] = 64.0**power * value

    for g in range(2):
        for there in range(0, ROWS // 2, 16):
            rows = slice(there + g * ROWS // 2, there + g * ROWS // 2 + 16)
            piece = roll(from_right_ref[there : there + 16, :], LB - 1 - 64 * g)
            for t in range(4):
                out = own_ref[t, rows, :]
                if t > 0:
                    at = LB - 1 + 16 * (t - 1)
                    out = out + jnp.where((lane16 >= at) & (lane16 < at + EDGE), piece, 0.0)
                b_ref[t, rows, :] = out * jnp.concatenate([inside[t]] * 2, axis=0)

    zeros = jnp.zeros((8, 128), F32)
    for t in range(4):
        for ref in (ve_ref, vo_ref, ve2_ref, vo2_ref, p_ref):
            ref[t, 0:8, :] = zeros
            ref[t, HI : HI + 8, :] = zeros
        for ref in (x_ref, x2_ref):
            for n in range(4):
                ref[n, t, 0:8, :] = zeros
                ref[n, t, HI : HI + 8, :] = zeros

    block_of = {}
    for block, (low, high) in enumerate(block_row_ranges()):
        for start in range(low, high, 8):
            block_of[start] = block

    def stages(src_ref, dst_ref, dst_shift, spread_refs, x_ref, y_refs, t_ref):
        def columns_out(start):
            rows = slice(start, start + 8)
            v = [src_ref[t, rows, :] for t in range(4)]
            before, after, second = lane_shift(v, -1), lane_shift(v, 1), lane_shift(v, 2)
            for t in range(4):
                spread_refs[0][t, rows, :] = 4.0 * v[t] + (before[t] + after[t])
                spread_refs[1][t, rows, :] = (before[t] + second[t]) + 23.0 * (v[t] + after[t])

        def rows_out(start):
            rows = slice(start, start + 8)
            block = block_of[start]
            for t in range(4):
                weights = [w_ref[power, t, 8 * block : 8 * block + 8, :] for power in range(3)]
                for n, ref in enumerate(spread_refs):
                    before = ref[t, start - 1 : start + 7, :]
                    here = ref[t, rows, :]
                    after = ref[t, start + 1 : start + 9, :]
                    second = ref[t, start + 2 : start + 10, :]
                    x_ref[2 * n, t, rows, :] = (4.0 * here + (before + after)) * weights[2 - n]
                    x_ref[2 * n + 1, t, rows, :] = ((before + second) + 23.0 * (here + after)) * weights[1 - n]

        def rows_in(start):
            for t in range(4):
                for n, ref in enumerate(y_refs):
                    ref[t, start : start + 8, :] = tap_rows(
                        lambda at, size: x_ref[2 * n, t, at : at + size, :],
                        lambda at, size: x_ref[2 * n + 1, t, at : at + size, :],
                        start,
                        8,
                    )

        def columns_part(start):
            rows = slice(start, start + 8)
            odd = [y_refs[1][t, rows, :] for t in range(4)]
            odd_before = lane_shift(odd, -1)
            for t in range(4):
                t_ref[t, rows, :] = y_refs[0][t, rows, :] + 23.0 * odd[t] + odd_before[t]

        def columns_in(start):
            rows = slice(start, start + 8)
            even = [y_refs[0][t, rows, :] for t in range(4)]
            odd = [y_refs[1][t, rows, :] for t in range(4)]
            first = lane_shift([t_ref[t, rows, :] for t in range(4)], -1)
            last = lane_shift([even[t] + odd[t] for t in range(4)], 1)
            for t in range(4):
                total = 4.0 * even[t] + 23.0 * odd[t] + first[t] + last[t]
                value = (total + ridge_weight * src_ref[t, rows, :]) * inside[t]
                dst_ref[t, start - dst_shift : start - dst_shift + 8, :] = value

        return [columns_out, rows_out, rows_in, columns_part, columns_in]

    work = [(stage, LO, HI) for stage in stages(b_ref, p_ref, 0, (ve_ref, vo_ref), x_ref, (ye_ref, yo_ref), t_ref)]
    second = stages(p_ref, s_ref, PAD, (ve2_ref, vo2_ref), x2_ref, (ye2_ref, yo2_ref), t2_ref)
    work += [(stage, LO, HI) for stage in second[:2]] + [(stage, PAD, PAD + 256) for stage in second[2:]]
    for step in range((HI - LO) // 8 + len(work) - 1):
        for n, (stage, low, high) in enumerate(work):
            start = LO + 8 * (step - n)
            if low <= start < high:
                stage(start)

    def total(x):
        return jnp.sum(jnp.sum(x, axis=0, keepdims=True), axis=1, keepdims=True)

    sums = [zeros, zeros]
    for t in range(4):
        for start in range(PAD, PAD + 256, 8):
            b = b_ref[t, start : start + 8, :] * main[t]
            p = p_ref[t, start : start + 8, :]
            sums = [sums[0] + b * b, sums[1] + b * p]
    norm, moment = total(sums[0]), total(sums[1])
    shift = jnp.where(norm > 1e-30, moment / jnp.where(norm > 1e-30, norm, 1.0), 0.0)
    shift8 = jnp.broadcast_to(shift, (8, 128))
    sums = [zeros] * 4
    for t in range(4):
        for start in range(PAD, PAD + 256, 8):
            b = b_ref[t, start : start + 8, :] * main[t]
            p = p_ref[t, start : start + 8, :] * main[t]
            s = s_ref[t, start - PAD : start - PAD + 8, :]
            w = p - shift8 * b
            z = s - shift8 * p
            sums = [sums[0] + w * b, sums[1] + w * w, sums[2] + w * z, sums[3] + b * z]
    values = [norm, moment] + [total(x) for x in sums] + [shift]
    row_lane = lax.broadcasted_iota(jnp.int32, (1, 8), 1)
    row = jnp.zeros((1, 8), F32)
    for n, value in enumerate(values):
        row = jnp.where(row_lane == n, jnp.broadcast_to(value, (1, 8)), row)
    red_ref[...] = jnp.broadcast_to(row, red_ref.shape)


def edge_slot(strip, start):
    if strip < 8:
        return start % 128, 16 * strip + 8 * (start // 128)
    return 128, start // 2


def edges_kernel(b_ref, p_ref, s_ref, out_ref):
    lane = lanes(16)
    places = {}
    for n, (src, base) in enumerate(((b_ref, PAD), (p_ref, PAD), (s_ref, 0))):
        for k in range(KS):
            for start in range(0, 256, 16):
                row, at = edge_slot(KS * n + k, start)
                places.setdefault(row, []).append((src, k, base + start, at))
    for row, pieces in places.items():
        out = jnp.zeros((16, 128), F32)
        for src, k, start, at in pieces:
            piece = roll(src[k + 1, start : start + 16, :], at - (LB + 16 * k))
            out = jnp.where((lane >= at) & (lane < at + SHIFT), piece, out)
        out_ref[row : row + 16, :] = out


def unpack_kernel(b_ref, p_ref, s_ref, bm_ref, pm_ref, sm_ref):
    lane = lanes(16)
    for src, dst, base in ((b_ref, bm_ref, PAD), (p_ref, pm_ref, PAD), (s_ref, sm_ref, 0)):
        for k in range(KS):
            off = LB + 16 * k
            for start in range(0, 256, 16):
                first = src[k, base + start : base + start + 16, :]
                second = src[k + 1, base + start : base + start + 16, :]
                dst[k, start : start + 16, :] = roll(jnp.where(lane >= off, first, second), -off)


def merge_kernel(edge_ref, b_ref, p_ref, s_ref, bm_ref, pm_ref, sm_ref):
    own = (lanes(16) >= SHIFT) | (lax.axis_index("axial") == 0)
    for n, (src, dst) in enumerate(((b_ref, bm_ref), (p_ref, pm_ref), (s_ref, sm_ref))):
        for k in range(KS):
            for start in range(0, 256, 16):
                rows = slice(start, start + 16)
                row, at = edge_slot(KS * n + k, start)
                dst[k, rows, :] = jnp.where(own, src[k, rows, :], roll(edge_ref[row : row + 16, :], -at))


def finish_kernel(red_ref, b_ref, p_ref, s_ref, sol_hbm, res_hbm, sol_ref, res_ref, sems):
    red = red_ref[...]
    mu = red[:, 6:7]

    def total(x):
        x = jnp.sum(x, axis=0, keepdims=True)
        return [x[:, n : n + 1] for n in range(6)]

    sums = jnp.sum(red, axis=0, keepdims=True)
    norm_now, moment_all = sums[:, 0:1], sums[:, 1:2]
    step = norm_now / moment_all
    shift = mu - moment_all / norm_now
    shifted = shift * red
    _, _, _, v, wz, bz = total(red)
    _, moment_1, c_1, v_1, _, bz_1 = total(shifted)
    norm_2, moment_2 = total(shift * shifted)[:2]
    c_mu = total(mu * red)[2]
    c_mu_1 = total(mu * shifted)[2]
    norm_next = step * step * (v + 2.0 * c_1 + norm_2)
    beta = norm_next / norm_now
    r_ar = step * step * (wz + v_1 + c_mu_1 + bz_1 + moment_2)
    cross = -step * (bz + v + c_mu + 2.0 * moment_1)
    curve = r_ar + beta * cross + beta * beta * moment_all
    step_two = norm_next / curve

    def wide(x):
        return jnp.broadcast_to(x, (16, 128))

    one_beta = 1.0 + beta
    step_b, step_two_b, one_beta_b = wide(step), wide(step_two), wide(one_beta)
    copies = []
    for k in range(KS):
        for start in range(0, 256, 16):
            rows = slice(start, start + 16)
            b, p, s = b_ref[k, rows, :], p_ref[k, rows, :], s_ref[k, rows, :]
            first = step_b * p
            sol_ref[k, rows, :] = step_b * b + step_two_b * (one_beta_b * b - first)
            res_ref[k, rows, :] = (b - first) - step_two_b * (one_beta_b * p - step_b * s)
        for n, (src, dst) in enumerate(((sol_ref, sol_hbm), (res_ref, res_hbm))):
            copies.append(pltpu.make_async_copy(src.at[k], dst.at[k], sems.at[2 * k + n]))
            copies[-1].start()
    for copy in copies:
        copy.wait()


def call(kernel, outs, scratch=(), n_in=1, cost=None, hbm_in=False, hbm_out=False, flag=False):
    vmem, hbm = pl.BlockSpec(memory_space=pltpu.VMEM), pl.BlockSpec(memory_space=pltpu.HBM)
    out_shape = [jax.ShapeDtypeStruct(shape, F32) for shape in outs]
    out_specs = [hbm if hbm_out else vmem] * len(outs)
    if flag:
        out_shape.append(jax.ShapeDtypeStruct((1,), jnp.int32))
        out_specs.append(pl.BlockSpec(memory_space=pltpu.SMEM))
    return pl.pallas_call(
        kernel,
        out_shape=out_shape,
        in_specs=[hbm if hbm_in else vmem] * n_in,
        out_specs=out_specs,
        scratch_shapes=[pltpu.VMEM(shape, F32) if isinstance(shape, tuple) else shape for shape in scratch],
        compiler_params=pltpu.CompilerParams(vmem_limit_bytes=VMEM_LIMIT),
        cost_estimate=cost,
    )


PACK_SCRATCH = [
    pltpu.VMEM((2, 4), jnp.int32),
    (KS, 1024, 128),
    (512, 128),
    (512, 128),
    pltpu.SemaphoreType.DMA((KS + 1,)),
]
FINISH_SCRATCH = [(KS, 256, 128), (KS, 256, 128), pltpu.SemaphoreType.DMA((2 * KS,))]
OPERATE_SCRATCH = [(3, 4, 48, 128)] + 2 * ([(4, ROWS, 128)] * 2 + [(4, 4, ROWS, 128)] + [(4, ROWS, 128)] * 3)


def shards(scanned, block_mask):
    x = pltpu.with_memory_space_constraint(scanned.reshape(KS, 1024, 128), pltpu.HBM)
    mask = pltpu.with_memory_space_constraint(block_mask.T, pltpu.HBM)
    (packed,) = call(pack_kernel, [(QN * PR, 128)], PACK_SCRATCH, n_in=2, hbm_in=True)(mask, x)
    got = lax.all_to_all(packed.reshape(QN, PR, 128), "circ", 0, 0, tiled=True).reshape(QN * PR, 128)
    b_own, to_left, mask_cols = call(
        collect_kernel,
        [(4, ROWS, 128), (ROWS // 2, 128), (8, 128)],
        [(4, ROWS, 128), (4, ROWS, 128)],
    )(got)
    from_right = lax.ppermute(to_left, "axial", [(i + 1, i) for i in range(AN - 1)])
    cost = pl.CostEstimate(flops=2_000_000, bytes_accessed=4_000_000, transcendentals=0)
    own, flag = call(place_kernel, [(4, ROWS, 128)], n_in=1, cost=cost, flag=True)(b_own)
    red, b, p, s = call(
        operate_kernel,
        [(QN * AN, 8), (4, ROWS, 128), (4, ROWS, 128), (4, 256, 128)],
        OPERATE_SCRATCH,
        n_in=3,
    )(own, mask_cols, from_right)
    all_red = lax.all_to_all(red, ("circ", "axial"), 0, 0, tiled=True)

    def share(b, p, s):
        (edges,) = call(edges_kernel, [(144, 128)], n_in=3, cost=cost)(b, p, s)
        edge = lax.ppermute(edges, "axial", [(i, i + 1) for i in range(AN - 1)])
        parts = call(unpack_kernel, [(KS, 256, 128)] * 3, n_in=3, cost=cost)(b, p, s)
        return tuple(call(merge_kernel, [(KS, 256, 128)] * 3, n_in=4, cost=cost)(edge, *parts))

    def keep(b, p, s):
        return tuple(x[:KS, :256] for x in (b, p, s))

    bm, pm, sm = lax.cond(flag[0] > 0, share, keep, b, p, s)
    return tuple(call(finish_kernel, [(KS, 256, 128)] * 2, FINISH_SCRATCH, n_in=4, hbm_out=True)(all_red, bm, pm, sm))


def solution(mesh):
    return jax.shard_map(
        shards,
        mesh=mesh,
        in_specs=(P(None, None, "circ", "axial"), P("circ", "axial")),
        out_specs=(P(None, "circ", "axial"), P(None, "circ", "axial")),
        check_vma=False,
    )
```

```python
import functools

import jax
import jax.numpy as jnp
from jax import lax
from jax.experimental import pallas as pl
from jax.experimental.pallas import tpu as pltpu
from jax.sharding import PartitionSpec as P

ridge_weight = 0.05
KS = 3
QN = 32
AN = 8
SL = 16
PR = 56
ROWS = 288
PAD = 16
LO, HI = 8, 280
LS, LB = 144, 2
SHIFT = 8
EDGE = 15
VMEM_LIMIT = 48 * 1024 * 1024
F32 = jnp.float32
BF16 = jnp.bfloat16


def column_matrix():
    sample = lax.broadcasted_iota(jnp.int32, (256, 256), 0)
    out = lax.broadcasted_iota(jnp.int32, (256, 256), 1)
    extra = out - 128
    extra = jnp.where(extra >= 18, extra - 18, extra)
    center = jnp.where(extra == 0, -2, jnp.where(extra < 3, 254 + 2 * extra, 120 + 2 * extra))
    center = jnp.where(out < 128, 2 * out, jnp.where(extra < 6, center, 1000))
    inner = (out >= 63) & (out <= 65) & (sample >= 128)
    outer = (out >= 128) & (extra >= 3) & (sample < 128)
    apart = inner | outer
    away = jnp.abs(sample - center)
    taps = jnp.where(away == 0, 32.0, jnp.where(away == 1, 23.0, jnp.where(away == 2, 8.0, 1.0)))
    return jnp.where((away > 3) | apart, 0.0, taps).astype(BF16)


def lanes(rows):
    return lax.broadcasted_iota(jnp.int32, (rows, 128), 1)


def roll(x, shift, axis=1):
    shift = shift % x.shape[axis]
    return x if shift == 0 else pltpu.roll(x, shift, axis)


def split_dot(x, matrix):
    high = x.astype(BF16)
    rest = x - high.astype(F32)
    mid = rest.astype(BF16)
    low = (rest - mid.astype(F32)).astype(BF16)
    dot = functools.partial(jnp.dot, preferred_element_type=F32)
    return dot(low, matrix) + dot(mid, matrix) + dot(high, matrix)


def pack_kernel(mask_hbm, x_hbm, out_ref, mask_ref, x_ref, main_ref, ext_ref, sems):
    q = lax.axis_index("circ")
    copies = [pltpu.make_async_copy(x_hbm.at[k], x_ref.at[k], sems.at[k]) for k in range(KS)]
    copies.append(pltpu.make_async_copy(mask_hbm, mask_ref, sems.at[KS]))
    for copy in copies:
        copy.start()
    lane = lanes(QN)
    matrix = column_matrix()
    tile = None
    ext17 = None
    next_rows = []
    for k in range(KS):
        copies[k].wait()
        left = x_ref[k, pl.ds(0, 512, stride=2), :]
        right = x_ref[k, pl.ds(1, 512, stride=2), :]
        both = split_dot(jnp.concatenate([left, right], axis=1), matrix)
        main_ref[...] = both[:, :128]
        ext_ref[...] = both[:, 128:]
        for d in range(QN):
            out_ref[pl.ds(d * PR + k * SL, SL), :] = both[d * SL : (d + 1) * SL, :128]
        ext = both[:, 128:].reshape(QN, 2, 8, 128)
        ext = jnp.where(lanes(QN * 8) < 18, ext[:, 0].reshape(QN * 8, 128), ext[:, 1].reshape(QN * 8, 128))
        ext = roll(ext, 6 * k)
        tile = ext if tile is None else tile + ext

        def neighbour(ref):
            first = ref[pl.ds(0, QN, stride=SL), :]
            last = ref[pl.ds(SL - 1, QN, stride=SL), :]
            return jnp.where(q >= QN // 2, roll(last, 1, 0), roll(first, -1, 0))

        next_rows.append(neighbour(main_ref))
        ext_row = roll(jnp.where(lane < 6, neighbour(ext_ref), 0.0), 6 * k)
        ext17 = ext_row if ext17 is None else ext17 + ext_row
    for d in range(QN):
        out_ref[pl.ds(d * PR + 48, 8), :] = tile[d * 8 : (d + 1) * 8]
    copies[KS].wait()
    mask = mask_ref[...].astype(F32)
    mask_row = jnp.zeros((1, 128), F32)
    for row in range(4):
        for col in range(2):
            value = jnp.broadcast_to(mask[col : col + 1, row : row + 1], (1, 128))
            mask_row = jnp.where(lanes(1) == 64 + 2 * row + col, value, mask_row)
    mask_row = jnp.broadcast_to(mask_row, (QN, 128))
    fill = []
    for k in range(KS):
        fill += [roll(next_rows[k], 64), next_rows[k]]
    fill += [roll(ext17, 64), mask_row]
    for row in range(8):
        where = pl.ds(48 + row, QN, stride=PR)
        out_ref[where, :] = jnp.where(lane < 64, out_ref[where, :], fill[row])


def tap_rows(even, odd, start, size):
    def ev(offset):
        return even(start + offset, size)

    def od(offset):
        return odd(start + offset, size)

    return (
        4.0 * ev(0) + (ev(-1) + ev(1)) + 23.0 * (od(-1) + od(0)) + (od(-2) + od(1))
    )


def block_row_ranges():
    edges = [LO] + [PAD + 64 * b for b in range(5)] + [HI]
    return list(zip(edges[:-1], edges[1:]))


def collect_kernel(got_ref, b_ref, left_ref, m_ref, even_ref, odd_ref):
    d = lax.axis_index("circ")
    row_lane = lanes(1)

    def spread_lane(x, at):
        return jnp.broadcast_to(x[:, at : at + 1], (1, 128))

    before = got_ref[pl.ds(lax.rem(d + QN - 1, QN) * PR + 55, 1), :]
    after = got_ref[pl.ds(lax.rem(d + 1, QN) * PR + 55, 1), :]
    weights = [(spread_lane(before, 70), spread_lane(before, 71))]
    mine = got_ref[pl.ds(d * PR + 55, 1), :]
    for row in range(4):
        weights.append(tuple(spread_lane(mine, 64 + 2 * row + col) for col in range(2)))
    weights.append((spread_lane(after, 64), spread_lane(after, 65)))
    all_main_w = [jnp.where(row_lane <= 65, low, high) for low, high in weights]
    ext_first = (row_lane == 0) | (row_lane == 6) | (row_lane == 12)
    all_ext_w = [jnp.where(ext_first, low, high) for low, high in weights]
    zeros = jnp.zeros((8, 128), F32)
    for ref in (even_ref, odd_ref):
        for t in range(4):
            ref[t, 0:8, :] = zeros
            ref[t, HI : HI + 8, :] = zeros
    for parity, ref in ((0, even_ref), (1, odd_ref)):
        if parity == 0:
            main_w, ext_w = [8.0 * w for w in all_main_w], [8.0 * w for w in all_ext_w]
        else:
            main_w, ext_w = all_main_w, all_ext_w
        for k in range(KS):
            for s in range(SL):
                rows = got_ref[pl.ds(parity * PR + k * SL + s, 16, stride=2 * PR), :]
                ref[k, PAD + 16 * s : PAD + 16 * s + 16, :] = rows * main_w[1 + s // 4]
            low = got_ref[pl.ds(parity * PR + 48 + 2 * k, 16, stride=2 * PR), :]
            high = got_ref[pl.ds(parity * PR + 49 + 2 * k, 16, stride=2 * PR), :]
            rows = jnp.where(lanes(16) < 64, roll(low, 64), high)
            ref[k, HI - 8 : HI, :] = rows[:8] * main_w[5]
            ref[k, LO : LO + 8, :] = rows[8:] * main_w[0]
        for r in range(8):
            rows = got_ref[pl.ds(parity * PR + 48 + r, 16, stride=2 * PR), :]
            ref[3, PAD + 16 * r : PAD + 16 * r + 16, :] = rows * ext_w[1 + r // 4]
            at = PAD + 128 + 16 * r
            ref[3, at : at + 16, :] = roll(rows, -18) * ext_w[3 + r // 4]
        rows = roll(got_ref[pl.ds(parity * PR + 54, 16, stride=2 * PR), :], 64)
        ref[3, HI - 8 : HI, :] = rows[:8] * ext_w[5]
        ref[3, LO : LO + 8, :] = rows[8:] * ext_w[0]
    scale = 1.0 / (48.0 * 48.0)
    for t in range(4):
        b_ref[t, 0:8, :] = zeros
        b_ref[t, HI : HI + 8, :] = zeros
        for start in range(LO, HI, 16):
            b_ref[t, start : start + 16, :] = scale * tap_rows(
                lambda at, size: even_ref[t, at : at + size, :],
                lambda at, size: odd_ref[t, at : at + size, :],
                start,
                16,
            )
    lane8 = lanes(8)
    mask_cols = jnp.zeros((8, 128), F32)
    sub8 = lax.broadcasted_iota(jnp.int32, (8, 128), 0)
    for row in range(6):
        for col in range(2):
            mask_cols = jnp.where((sub8 == row) & (lane8 == 24 + col), weights[row][col], mask_cols)
    m_ref[...] = mask_cols
    first_col = jnp.zeros((8, 128), F32)
    for row in range(6):
        first_col = jnp.where((sub8 == row) & (lane8 == EDGE), weights[row][0], first_col)
    lane16 = lanes(16)
    for start in range(0, ROWS // 2, 16):
        halves = []
        for g in range(2):
            rows = slice(start + g * ROWS // 2, start + g * ROWS // 2 + 16)
            ext = b_ref[3, rows, :]
            piece = jnp.zeros((16, 128), F32)
            for k in range(KS):
                at = 16 * k
                piece = jnp.where(lane16 == at, roll(ext, at - 6 * k), piece)
                piece = jnp.where((lane16 > at) & (lane16 < at + EDGE), roll(b_ref[k, rows, :], at + 1), piece)
            halves.append(piece)
        out = halves[0] + roll(halves[1], 64)
        if start == 0:
            out = out + jnp.concatenate([first_col, zeros], axis=0)
        left_ref[start : start + 16, :] = out


def place_kernel(b_ref, out_ref, flag_ref):
    flag_ref[0] = 1
    lane = lanes(16)
    for t in range(4):
        for start in range(0, ROWS, 16):
            rows = slice(start, start + 16)
            out = jnp.zeros((16, 128), F32)
            ext = b_ref[3, rows, :]
            if t > 0:
                off = LB + 16 * (t - 1)
                out = jnp.where(lane < off, roll(b_ref[t - 1, rows, :], off), out)
                piece = roll(ext, off - 1 - 6 * (t - 1))
                out = jnp.where((lane >= off) & (lane < off + 2), piece, out)
            if t < KS:
                off = LB + 16 * t
                out = jnp.where(lane >= off, roll(b_ref[t, rows, :], off), out)
                piece = roll(ext, off + 63 - (6 * t + 3))
                out = out + jnp.where((lane >= off + 63) & (lane < off + 66), piece, 0.0)
            out_ref[t, rows, :] = out


def lane_shift(parts, shift):
    rolled = [roll(part, -shift) for part in parts]
    lane = lanes(parts[0].shape[0])
    count = len(parts)
    if shift < 0:
        return [jnp.where(lane < -shift, rolled[(t - 1) % count], rolled[t]) for t in range(count)]
    return [jnp.where(lane >= 128 - shift, rolled[(t + 1) % count], rolled[t]) for t in range(count)]


def packed_columns(t):
    out = []
    for lane in range(128):
        at = 128 * t + lane
        k = min(at // LS, KS - 1)
        out.append(at - k * LS - LB)
    return out


def lane_range(lane, t, low, high):
    columns = packed_columns(t)
    where = None
    at = 0
    while at < 128:
        if low <= columns[at] < high:
            end = at
            while end < 128 and low <= columns[end] < high:
                end += 1
            piece = (lane >= at) & (lane < end)
            where = piece if where is None else where | piece
            at = end
        else:
            at += 1
    return where


def choose(where, x, y):
    return y if where is None else jnp.where(where, x, y)


def operate_kernel(
    own_ref,
    m_ref,
    from_right_ref,
    red_ref,
    b_ref,
    p_ref,
    s_ref,
    edge_ref,
    w_ref,
    ve_ref,
    vo_ref,
    x_ref,
    ye_ref,
    yo_ref,
    t_ref,
    ve2_ref,
    vo2_ref,
    x2_ref,
    ye2_ref,
    yo2_ref,
    t2_ref,
):
    place = lax.axis_index("axial")
    first_tile = (place == 0).astype(F32)
    inner_right = (place < AN - 1).astype(F32)
    lane8 = lanes(8)
    lane16 = lanes(16)
    ones = jnp.ones((8, 128), F32)
    inside = []
    main = []
    for t in range(4):
        keep = choose(lane_range(lane8, t, -LB, 0), jnp.zeros((8, 128), F32), ones)
        inside.append(choose(lane_range(lane8, t, 128, 400), ones * inner_right, keep))
        own = choose(lane_range(lane8, t, SHIFT, SHIFT + 128), ones, jnp.zeros((8, 128), F32))
        main.append(choose(lane_range(lane8, t, 0, SHIFT), ones * first_tile, own))
    scale = 1.0 / (48.0**4)
    for block in range(6):

        def cell(ref, at):
            return jnp.broadcast_to(ref[block : block + 1, at : at + 1], (8, 128)) * scale

        low, high = cell(m_ref, 24), cell(m_ref, 25)
        right = cell(from_right_ref, EDGE)
        for t in range(4):
            value = choose(lane_range(lane8, t, -LB, 0), jnp.zeros((8, 128), F32), right)
            value = choose(lane_range(lane8, t, 0, 64), low, value)
            value = choose(lane_range(lane8, t, 64, 128), high, value)
            for power in range(3):
                w_ref[power, t, 8 * block : 8 * block + 8, :] = 64.0**power * value

    for g in range(2):
        for there in range(0, ROWS // 2, 16):
            rows = slice(there + g * ROWS // 2, there + g * ROWS // 2 + 16)
            piece = roll(from_right_ref[there : there + 16, :], LB - 1 - 64 * g)
            for t in range(4):
                out = own_ref[t, rows, :]
                if t > 0:
                    at = LB - 1 + 16 * (t - 1)
                    out = out + jnp.where((lane16 >= at) & (lane16 < at + EDGE), piece, 0.0)
                b_ref[t, rows, :] = out * jnp.concatenate([inside[t]] * 2, axis=0)

    zeros = jnp.zeros((8, 128), F32)
    for t in range(4):
        for ref in (ve_ref, vo_ref, ve2_ref, vo2_ref, p_ref):
            ref[t, 0:8, :] = zeros
            ref[t, HI : HI + 8, :] = zeros
        for ref in (x_ref, x2_ref):
            for n in range(4):
                ref[n, t, 0:8, :] = zeros
                ref[n, t, HI : HI + 8, :] = zeros

    block_of = {}
    for block, (low, high) in enumerate(block_row_ranges()):
        for start in range(low, high, 8):
            block_of[start] = block

    def stages(src_ref, dst_ref, dst_shift, spread_refs, x_ref, y_refs, t_ref):
        def columns_out(start):
            rows = slice(start, start + 8)
            v = [src_ref[t, rows, :] for t in range(4)]
            before, after, second = lane_shift(v, -1), lane_shift(v, 1), lane_shift(v, 2)
            for t in range(4):
                spread_refs[0][t, rows, :] = 4.0 * v[t] + (before[t] + after[t])
                spread_refs[1][t, rows, :] = (before[t] + second[t]) + 23.0 * (v[t] + after[t])

        def rows_out(start):
            rows = slice(start, start + 8)
            block = block_of[start]
            for t in range(4):
                weights = [w_ref[power, t, 8 * block : 8 * block + 8, :] for power in range(3)]
                for n, ref in enumerate(spread_refs):
                    before = ref[t, start - 1 : start + 7, :]
                    here = ref[t, rows, :]
                    after = ref[t, start + 1 : start + 9, :]
                    second = ref[t, start + 2 : start + 10, :]
                    x_ref[2 * n, t, rows, :] = (4.0 * here + (before + after)) * weights[2 - n]
                    x_ref[2 * n + 1, t, rows, :] = ((before + second) + 23.0 * (here + after)) * weights[1 - n]

        def rows_in(start):
            for t in range(4):
                for n, ref in enumerate(y_refs):
                    ref[t, start : start + 8, :] = tap_rows(
                        lambda at, size: x_ref[2 * n, t, at : at + size, :],
                        lambda at, size: x_ref[2 * n + 1, t, at : at + size, :],
                        start,
                        8,
                    )

        def columns_part(start):
            rows = slice(start, start + 8)
            odd = [y_refs[1][t, rows, :] for t in range(4)]
            odd_before = lane_shift(odd, -1)
            for t in range(4):
                t_ref[t, rows, :] = y_refs[0][t, rows, :] + 23.0 * odd[t] + odd_before[t]

        def columns_in(start):
            rows = slice(start, start + 8)
            even = [y_refs[0][t, rows, :] for t in range(4)]
            odd = [y_refs[1][t, rows, :] for t in range(4)]
            first = lane_shift([t_ref[t, rows, :] for t in range(4)], -1)
            last = lane_shift([even[t] + odd[t] for t in range(4)], 1)
            for t in range(4):
                total = 4.0 * even[t] + 23.0 * odd[t] + first[t] + last[t]
                value = (total + ridge_weight * src_ref[t, rows, :]) * inside[t]
                dst_ref[t, start - dst_shift : start - dst_shift + 8, :] = value

        return [columns_out, rows_out, rows_in, columns_part, columns_in]

    work = [(stage, LO, HI) for stage in stages(b_ref, p_ref, 0, (ve_ref, vo_ref), x_ref, (ye_ref, yo_ref), t_ref)]
    second = stages(p_ref, s_ref, PAD, (ve2_ref, vo2_ref), x2_ref, (ye2_ref, yo2_ref), t2_ref)
    work += [(stage, LO, HI) for stage in second[:2]] + [(stage, PAD, PAD + 256) for stage in second[2:]]
    for step in range((HI - LO) // 8 + len(work) - 1):
        for n, (stage, low, high) in enumerate(work):
            start = LO + 8 * (step - n)
            if low <= start < high:
                stage(start)

    edges_kernel(b_ref, p_ref, s_ref, edge_ref)

    def total(x):
        return jnp.sum(jnp.sum(x, axis=0, keepdims=True), axis=1, keepdims=True)

    sums = [zeros, zeros]
    for t in range(4):
        for start in range(PAD, PAD + 256, 8):
            b = b_ref[t, start : start + 8, :] * main[t]
            p = p_ref[t, start : start + 8, :]
            sums = [sums[0] + b * b, sums[1] + b * p]
    norm, moment = total(sums[0]), total(sums[1])
    shift = jnp.where(norm > 1e-30, moment / jnp.where(norm > 1e-30, norm, 1.0), 0.0)
    shift8 = jnp.broadcast_to(shift, (8, 128))
    sums = [zeros] * 4
    for t in range(4):
        for start in range(PAD, PAD + 256, 8):
            b = b_ref[t, start : start + 8, :] * main[t]
            p = p_ref[t, start : start + 8, :] * main[t]
            s = s_ref[t, start - PAD : start - PAD + 8, :]
            w = p - shift8 * b
            z = s - shift8 * p
            sums = [sums[0] + w * b, sums[1] + w * w, sums[2] + w * z, sums[3] + b * z]
    values = [norm, moment] + [total(x) for x in sums] + [shift]
    row_lane = lax.broadcasted_iota(jnp.int32, (1, 8), 1)
    row = jnp.zeros((1, 8), F32)
    for n, value in enumerate(values):
        row = jnp.where(row_lane == n, jnp.broadcast_to(value, (1, 8)), row)
    red_ref[...] = jnp.broadcast_to(row, red_ref.shape)


def edge_slot(strip, start):
    if strip < 8:
        return start % 128, 16 * strip + 8 * (start // 128)
    return 128, start // 2


def edges_kernel(b_ref, p_ref, s_ref, out_ref):
    lane = lanes(16)
    places = {}
    for n, (src, base) in enumerate(((b_ref, PAD), (p_ref, PAD), (s_ref, 0))):
        for k in range(KS):
            for start in range(0, 256, 16):
                row, at = edge_slot(KS * n + k, start)
                places.setdefault(row, []).append((src, k, base + start, at))
    for row, pieces in places.items():
        out = jnp.zeros((16, 128), F32)
        for src, k, start, at in pieces:
            piece = roll(src[k + 1, start : start + 16, :], at - (LB + 16 * k))
            out = jnp.where((lane >= at) & (lane < at + SHIFT), piece, out)
        out_ref[row : row + 16, :] = out


def unpack_kernel(b_ref, p_ref, s_ref, bm_ref, pm_ref, sm_ref):
    lane = lanes(16)
    for src, dst, base in ((b_ref, bm_ref, PAD), (p_ref, pm_ref, PAD), (s_ref, sm_ref, 0)):
        for k in range(KS):
            off = LB + 16 * k
            for start in range(0, 256, 16):
                first = src[k, base + start : base + start + 16, :]
                second = src[k + 1, base + start : base + start + 16, :]
                dst[k, start : start + 16, :] = roll(jnp.where(lane >= off, first, second), -off)


def merge_kernel(edge_ref, b_ref, p_ref, s_ref, bm_ref, pm_ref, sm_ref):
    own = (lanes(16) >= SHIFT) | (lax.axis_index("axial") == 0)
    for n, (src, dst) in enumerate(((b_ref, bm_ref), (p_ref, pm_ref), (s_ref, sm_ref))):
        for k in range(KS):
            for start in range(0, 256, 16):
                rows = slice(start, start + 16)
                row, at = edge_slot(KS * n + k, start)
                dst[k, rows, :] = jnp.where(own, src[k, rows, :], roll(edge_ref[row : row + 16, :], -at))


def finish_kernel(red_ref, b_ref, p_ref, s_ref, sol_hbm, res_hbm, sol_ref, res_ref, sems):
    red = red_ref[...]
    mu = red[:, 6:7]

    def total(x):
        x = jnp.sum(x, axis=0, keepdims=True)
        return [x[:, n : n + 1] for n in range(6)]

    sums = jnp.sum(red, axis=0, keepdims=True)
    norm_now, moment_all = sums[:, 0:1], sums[:, 1:2]
    step = norm_now / moment_all
    shift = mu - moment_all / norm_now
    shifted = shift * red
    _, _, _, v, wz, bz = total(red)
    _, moment_1, c_1, v_1, _, bz_1 = total(shifted)
    norm_2, moment_2 = total(shift * shifted)[:2]
    c_mu = total(mu * red)[2]
    c_mu_1 = total(mu * shifted)[2]
    norm_next = step * step * (v + 2.0 * c_1 + norm_2)
    beta = norm_next / norm_now
    r_ar = step * step * (wz + v_1 + c_mu_1 + bz_1 + moment_2)
    cross = -step * (bz + v + c_mu + 2.0 * moment_1)
    curve = r_ar + beta * cross + beta * beta * moment_all
    step_two = norm_next / curve

    def wide(x):
        return jnp.broadcast_to(x, (16, 128))

    one_beta = 1.0 + beta
    step_b, step_two_b, one_beta_b = wide(step), wide(step_two), wide(one_beta)
    copies = []
    for k in range(KS):
        for start in range(0, 256, 16):
            rows = slice(start, start + 16)
            b, p, s = b_ref[k, rows, :], p_ref[k, rows, :], s_ref[k, rows, :]
            first = step_b * p
            sol_ref[k, rows, :] = step_b * b + step_two_b * (one_beta_b * b - first)
            res_ref[k, rows, :] = (b - first) - step_two_b * (one_beta_b * p - step_b * s)
        for n, (src, dst) in enumerate(((sol_ref, sol_hbm), (res_ref, res_hbm))):
            copies.append(pltpu.make_async_copy(src.at[k], dst.at[k], sems.at[2 * k + n]))
            copies[-1].start()
    for copy in copies:
        copy.wait()


def call(kernel, outs, scratch=(), n_in=1, cost=None, hbm_in=False, hbm_out=False, flag=False):
    vmem, hbm = pl.BlockSpec(memory_space=pltpu.VMEM), pl.BlockSpec(memory_space=pltpu.HBM)
    out_shape = [jax.ShapeDtypeStruct(shape, F32) for shape in outs]
    out_specs = [hbm if hbm_out else vmem] * len(outs)
    if flag:
        out_shape.append(jax.ShapeDtypeStruct((1,), jnp.int32))
        out_specs.append(pl.BlockSpec(memory_space=pltpu.SMEM))
    return pl.pallas_call(
        kernel,
        out_shape=out_shape,
        in_specs=[hbm if hbm_in else vmem] * n_in,
        out_specs=out_specs,
        scratch_shapes=[pltpu.VMEM(shape, F32) if isinstance(shape, tuple) else shape for shape in scratch],
        compiler_params=pltpu.CompilerParams(vmem_limit_bytes=VMEM_LIMIT),
        cost_estimate=cost,
    )


PACK_SCRATCH = [
    pltpu.VMEM((2, 4), jnp.int32),
    (KS, 1024, 128),
    (512, 128),
    (512, 128),
    pltpu.SemaphoreType.DMA((KS + 1,)),
]
FINISH_SCRATCH = [(KS, 256, 128), (KS, 256, 128), pltpu.SemaphoreType.DMA((2 * KS,))]
OPERATE_SCRATCH = [(3, 4, 48, 128)] + 2 * ([(4, ROWS, 128)] * 2 + [(4, 4, ROWS, 128)] + [(4, ROWS, 128)] * 3)


def shards(scanned, block_mask):
    x = pltpu.with_memory_space_constraint(scanned.reshape(KS, 1024, 128), pltpu.HBM)
    mask = pltpu.with_memory_space_constraint(block_mask.T, pltpu.HBM)
    (packed,) = call(pack_kernel, [(QN * PR, 128)], PACK_SCRATCH, n_in=2, hbm_in=True)(mask, x)
    got = lax.all_to_all(packed.reshape(QN, PR, 128), "circ", 0, 0, tiled=True).reshape(QN * PR, 128)
    b_own, to_left, mask_cols = call(
        collect_kernel,
        [(4, ROWS, 128), (ROWS // 2, 128), (8, 128)],
        [(4, ROWS, 128), (4, ROWS, 128)],
    )(got)
    from_right = lax.ppermute(to_left, "axial", [(i + 1, i) for i in range(AN - 1)])
    cost = pl.CostEstimate(flops=2_000_000, bytes_accessed=4_000_000, transcendentals=0)
    own, flag = call(place_kernel, [(4, ROWS, 128)], n_in=1, cost=cost, flag=True)(b_own)
    red, b, p, s, edges = call(
        operate_kernel,
        [(QN * AN, 8), (4, ROWS, 128), (4, ROWS, 128), (4, 256, 128), (144, 128)],
        OPERATE_SCRATCH,
        n_in=3,
    )(own, mask_cols, from_right)
    all_red = lax.all_to_all(red, ("circ", "axial"), 0, 0, tiled=True)

    def share(b, p, s, edges):
        edge = lax.ppermute(edges, "axial", [(i, i + 1) for i in range(AN - 1)])
        parts = call(unpack_kernel, [(KS, 256, 128)] * 3, n_in=3, cost=cost)(b, p, s)
        return tuple(call(merge_kernel, [(KS, 256, 128)] * 3, n_in=4, cost=cost)(edge, *parts))

    def keep(b, p, s, edges):
        return tuple(x[:KS, :256] for x in (b, p, s))

    bm, pm, sm = lax.cond(flag[0] > 0, share, keep, b, p, s, edges)
    return tuple(call(finish_kernel, [(KS, 256, 128)] * 2, FINISH_SCRATCH, n_in=4, hbm_out=True)(all_red, bm, pm, sm))


def solution(mesh):
    return jax.shard_map(
        shards,
        mesh=mesh,
        in_specs=(P(None, None, "circ", "axial"), P("circ", "axial")),
        out_specs=(P(None, "circ", "axial"), P(None, "circ", "axial")),
        check_vma=False,
    )
```
